512 devices in a mesh: dp: 64 (over z, x), cent: 8 (over y, core).
Axes of the slice: x: 4, y: 4, z: 16, core: 2. Of those that a mesh axis runs over, the one named last changes fastest.
Arguments:
- embeddings: float32 [98304, 1024], P(('dp', 'cent')), may hold values from -128 to 128
- centroids: float32 [4096, 1024], P(('dp', 'cent')), may hold values from -6 to 6
Outputs:
- updated: float32 [4096, 1024], P(('dp', 'cent'))
- entropy: float32 [98304], P(('dp', 'cent'))
The draws below stay inside these ranges and needn't reach their ends.
All inputs are finite; a program needn't handle non-finite values.
Results may differ from the reference program's by a relative error of at most 0.024.
Values may be sent and summed in bfloat16 or wider, within the bound.
A program may use at most 64 MiB of HBM per device.

```python
import math
import jax
import jax.numpy as jnp
from jax import lax

D = 1024
K = 4096
GROUP = 1536
ROWS = 98304


def shared_centroids(key):
    key = jax.random.fold_in(key, 301)
    return jnp.clip(jax.random.normal(key, (K, D), jnp.float32), -6.0, 6.0)


def draw_centroids(key, part):
    shared = shared_centroids(key)
    return shared


def draw_embeddings(key, part):
    shared = shared_centroids(key)
    key = jax.random.fold_in(key, 11)
    keys_all = jax.random.split(key, 8)
    key_noise = keys_all[0]
    key_rough = keys_all[1]
    key_single = keys_all[3]
    key_jitter = keys_all[4]
    key_first = keys_all[5]
    key_second = keys_all[6]
    key_margin = keys_all[7]
    position = jnp.arange(ROWS, dtype=jnp.float32) / ROWS
    noise = jnp.clip(jax.random.normal(key_noise, (ROWS, D), jnp.float32), -6.0, 6.0)
    rough = jnp.exp(jax.random.uniform(key_rough, (ROWS,), jnp.float32, 0.0, math.log(2.0)))
    scale = (1.0 + 2.0 * position) * rough
    drawn_rows = scale[:, None] * noise
    planted = ROWS // 32
    blocks = jnp.arange(planted, dtype=jnp.int32)
    single_pick = jax.random.randint(key_single, (planted,), 0, K)
    single_gain = (8 + 4 * (blocks % 4)).astype(jnp.float32)
    jitter = jnp.clip(jax.random.normal(key_jitter, (planted, D), jnp.float32), -6.0, 6.0)
    single_rows = single_gain[:, None] * shared[single_pick] + 0.5 * jitter
    first_pick = jax.random.randint(key_first, (planted,), 0, K)
    second_pick = (first_pick + jax.random.randint(key_second, (planted,), 1, K)) % K
    closer = shared[first_pick]
    farther = shared[second_pick]
    paired_improvement = (8 + 2 * (blocks % 3)).astype(jnp.float32)
    logit_margin = jax.random.uniform(key_margin, (planted,), jnp.float32, 1.5, 2.5)
    between = closer - farther
    norm_difference = jnp.sum(closer * closer - farther * farther, axis=1)
    separation_squared = jnp.sum(between * between, axis=1)
    logit_shift = (2.0 * sampled_softness() * logit_margin - (paired_improvement - 1.0) * norm_difference) / (2.0 * separation_squared)
    pair_rows = 0.5 * paired_improvement[:, None] * (closer + farther) + logit_shift[:, None] * between
    lattice = drawn_rows.reshape(planted, 32, D)
    lattice = lattice.at[:, 5, :].set(single_rows)
    lattice = lattice.at[:, 21, :].set(pair_rows)
    return jnp.clip(lattice.reshape(ROWS, D), -128.0, 128.0).astype(jnp.float32)


def sampled_softness():
    return 32.0


def setup_inputs(seed: int = 0) -> dict:
    arg_keys = jax.random.split(jax.random.key(seed), 3)
    embeddings = draw_embeddings(jax.random.fold_in(arg_keys[2], 71), 0)
    centroids = draw_centroids(jax.random.fold_in(arg_keys[2], 71), 0)
    return dict(embeddings=embeddings, centroids=centroids)


softness_level = 32.0
prior_mass = 4.0


def to_bf(values):
    return lax.optimization_barrier(values.astype(jnp.bfloat16)).astype(jnp.float32)


def scores_of(rows, row_norms, cents, centroid_norm):
    inner_products = jnp.dot(rows, cents.T, precision=lax.Precision.HIGHEST, preferred_element_type=jnp.float32)
    return -(row_norms[:, None] - 2.0 * inner_products + centroid_norm[None, :]) / (2.0 * softness_level)


def reference(embeddings, centroids):
    rows_b = to_bf(embeddings)
    row_squared_norm = jnp.sum(rows_b * rows_b, axis=1)
    row_blocks = rows_b.reshape(ROWS // GROUP, GROUP, D)
    norm_blocks = row_squared_norm.reshape(ROWS // GROUP, GROUP)
    cent_b = to_bf(centroids)
    centroid_squared_norm = jnp.sum(cent_b * cent_b, axis=1)

    def accumulate(carry, item):
        rows, row_norms = item
        score = scores_of(rows, row_norms, cent_b, centroid_squared_norm)
        top = jnp.max(score, axis=1)
        weight = jnp.exp(score - top[:, None])
        total = jnp.sum(weight, axis=1)
        resp = to_bf(weight / total[:, None])
        sums = carry[0] + jnp.dot(resp.T, rows, precision=lax.Precision.HIGHEST, preferred_element_type=jnp.float32)
        counts = carry[1] + jnp.sum(resp, axis=0)
        return (sums, counts), 0.0

    start = (jnp.zeros((K, D), jnp.float32), jnp.zeros((K,), jnp.float32))
    (sums, counts), unused = lax.scan(accumulate, start, (row_blocks, norm_blocks))
    updated = (sums + prior_mass * centroids) / (counts + prior_mass)[:, None]
    new_b = to_bf(updated)
    new_sq = jnp.sum(new_b * new_b, axis=1)

    def entropy_block(item):
        rows, row_norms = item
        score = scores_of(rows, row_norms, new_b, new_sq)
        top = jnp.max(score, axis=1)
        shifted = score - top[:, None]
        weight = jnp.exp(shifted)
        total = jnp.sum(weight, axis=1)
        spread = jnp.sum(weight * shifted, axis=1)
        return jnp.log(total) - spread / total

    entropy = lax.map(entropy_block, (row_blocks, norm_blocks)).reshape(ROWS)
    return updated, entropy
```

```python
import jax
import jax.numpy as jnp
from jax import lax
from jax.experimental import pallas as pl
from jax.experimental.pallas import tpu as pltpu
from jax.sharding import PartitionSpec as P

MESH = pl.DeviceIdType.MESH
F32 = jnp.float32
BF16 = jnp.bfloat16

softness_level = 32.0
prior_mass = 4.0

D = 1024
NZ, NX, NY, NC = 16, 4, 4, 2
NCENT = NY * NC
ROWS = 192
GROUP = ROWS * NCENT
CHIP = ROWS * NC
OWN = 8
SLICE = OWN * NZ * NX
PARTS = 4
W = D // (2 * PARTS)
LANES = 128
TILES = GROUP // LANES
CHIP_TILES = CHIP // LANES
SCALE = 2.0 * softness_level


def place():
    dp = lax.axis_index("dp")
    cent = lax.axis_index("cent")
    z = dp // NX
    x = dp % NX
    y = cent // NC
    core = cent % NC
    return z, x, y, core, cent


def far_first(step):
    half = (step + 1) // 2
    return NZ // 2 + half * (1 - 2 * (step % 2))


def kernel(
    emb_hbm,
    cent_hbm,
    upd_out,
    ent_out,
    emb_v,
    cent_v,
    rows,
    first,
    second,
    operand,
    norm_part,
    norm,
    row_sq,
    acc,
    resp,
    stat_send,
    stat_recv,
    factor,
    stat2_send,
    stat2_recv,
    sums_f,
    sums_send,
    sums_recv,
    part_send,
    part_recv,
    count_send,
    count_recv,
    total_send,
    total_recv,
    load_sem,
    rows_send_sem,
    rows_recv_sem,
    gz_send,
    gz_recv,
    gx_send,
    gx_recv,
    st_send,
    st_recv,
    cx_send,
    cx_recv,
    cz_send,
    cz_recv,
    nx_send,
    nx_recv,
    nz_send,
    nz_recv,
    uz_send,
    uz_recv,
    ux_send,
    ux_recv,
    st2_send,
    st2_recv,
):
    z, x, y, core, cent = place()

    def at_zx(z_to, x_to):
        return {"dp": z_to * NX + x_to, "cent": cent}

    def at_cent(cent_to):
        return {"dp": z * NX + x, "cent": cent_to}

    def remote(src, dst, send, recv, device):
        return pltpu.make_async_remote_copy(
            src_ref=src, dst_ref=dst, send_sem=send, recv_sem=recv, device_id=device, device_id_type=MESH
        )

    def take(ref, sem):
        pltpu.make_async_copy(ref, ref, sem).wait()

    load_cent = pltpu.make_async_copy(cent_hbm, cent_v, load_sem.at[0])
    load_emb = pltpu.make_async_copy(emb_hbm, emb_v, load_sem.at[1])
    load_cent.start()
    load_emb.start()

    barrier = pltpu.get_barrier_semaphore()

    def greet_z(step, carry):
        pl.semaphore_signal(
            barrier, inc=1, device_id=at_zx((z + far_first(step)) % NZ, x), device_id_type=MESH
        )
        return carry

    lax.fori_loop(0, NZ - 1, greet_z, 0)
    for k in range(1, NCENT):
        pl.semaphore_signal(
            barrier, inc=1, device_id=at_cent((cent + k) % NCENT), device_id_type=MESH
        )
    for k in range(1, NX):
        pl.semaphore_signal(barrier, inc=1, device_id=at_zx(z, (x + k) % NX), device_id_type=MESH)

    load_cent.wait()
    for p in range(PARTS):
        left = cent_v[:, 2 * W * p : 2 * W * p + W]
        right = cent_v[:, 2 * W * p + W : 2 * W * (p + 1)]
        first[p, x, z] = jnp.concatenate([left, right], axis=0).astype(BF16)
    load_emb.wait()
    own_rows = pl.ds(pl.multiple_of(cent * ROWS, ROWS), ROWS)
    rows[own_rows, :] = emb_v[...].astype(BF16)

    pl.semaphore_wait(barrier, (NZ - 1) + (NCENT - 1) + (NX - 1))

    def spread_z(buf, p, send, recv):
        def go(step, carry):
            remote(
                buf.at[p, x, z],
                buf.at[p, x, z],
                send.at[p],
                recv.at[p],
                at_zx((z + far_first(step)) % NZ, x),
            ).start()
            return carry

        lax.fori_loop(0, NZ - 1, go, 0)

    def spread_x(buf, p, send, recv):
        take(buf.at[p, x, pl.ds(0, NZ - 1)], recv[0].at[p])
        for k in (2, 1, 3):
            remote(
                buf.at[p, x], buf.at[p, x], send.at[p], recv[1].at[p], at_zx(z, (x + k) % NX)
            ).start()

    def each_part(body):
        def go(p, carry):
            body(p)
            return carry

        lax.fori_loop(0, PARTS, go, 0)

    each_part(lambda p: spread_z(first, p, gz_send, gz_recv))

    def row_copy(owner, device, send):
        block = pl.ds(pl.multiple_of(owner * ROWS, ROWS), ROWS)
        return remote(
            rows.at[block, :], rows.at[block, :], rows_send_sem.at[send], rows_recv_sem.at[owner], device
        )

    sibling = at_cent(y * NC + 1 - core)
    for send, k in enumerate((1, 3, 2)):
        row_copy(cent, at_cent(((y + k) % NY) * NC + core), send).start()
    row_copy(cent, sibling, 3).start()

    each_part(lambda p: spread_x(first, p, gx_send, (gz_recv, gx_recv)))

    for send, k in enumerate((1, 3, 2)):
        owner = ((y + k) % NY) * NC + core
        row_copy(owner, sibling, send).wait_recv()
        row_copy(owner, sibling, 4 + send).start()
    for k in range(NY):
        row_copy(((y + k) % NY) * NC + 1 - core, sibling, 0).wait_recv()

    def row_norms(j, carry):
        here = pl.ds(pl.multiple_of(j * LANES, LANES), LANES)
        part = jnp.zeros((LANES, LANES), F32)
        for i in range(D // LANES):
            block = rows[here, i * LANES : (i + 1) * LANES].astype(F32)
            part += block * block
        row_sq[:, here] = jnp.sum(part.T, axis=0, keepdims=True)
        return carry

    lax.fori_loop(0, TILES, row_norms, 0)

    def products(buf, recv):
        def part(p):
            take(buf.at[p, pl.ds(0, NX - 1)], recv.at[p])
            lo = pl.ds(pl.multiple_of(2 * W * p, 2 * W), W)
            hi = pl.ds(pl.multiple_of(2 * W * p + W, W), W)
            both = pl.ds(pl.multiple_of(2 * W * p, 2 * W), 2 * W)
            for i in range(NX):
                block = buf[p, i].astype(F32)
                left = block[:, :OWN].reshape(NZ * OWN, W)
                right = block[:, OWN:].reshape(NZ * OWN, W)
                here = slice(i * NZ * OWN, (i + 1) * NZ * OWN)
                operand[here, lo] = left.astype(BF16)
                operand[here, hi] = right.astype(BF16)
                square = left * left + right * right
                norm_part[here, :] = jnp.where(p == 0, square, norm_part[here, :] + square)

            def tile(t, carry):
                here = pl.ds(pl.multiple_of(t * 256, 256), 256)
                piece = lax.dot_general(
                    operand[:, both],
                    rows[here, both],
                    (((1,), (1,)), ((), ())),
                    preferred_element_type=F32,
                )
                acc[:, here] = jnp.where(p == 0, piece, acc[:, here] + piece)
                return carry

            lax.fori_loop(0, GROUP // 256, tile, 0)

        norm_part[...] = jnp.zeros_like(norm_part)
        acc[...] = jnp.zeros_like(acc)
        each_part(part)
        norm[...] = jnp.broadcast_to(
            jnp.sum(norm_part[...], axis=1, keepdims=True), (SLICE, LANES)
        )

    def score_tile(t):
        here = pl.ds(pl.multiple_of(t * LANES, LANES), LANES)
        return here, -(row_sq[:, here] - 2.0 * acc[:, here] + norm[...]) / SCALE

    products(first, gx_recv)

    def first_stats(t, carry):
        here, score = score_tile(t)
        top = jnp.max(score, axis=0, keepdims=True)
        weight = jnp.exp(score - top)
        acc[:, here] = weight
        stat_send[t // 4, pl.ds(t % 4, 1), :] = top
        stat_send[t // 4, pl.ds(4 + t % 4, 1), :] = jnp.sum(weight, axis=0, keepdims=True)
        return carry

    lax.fori_loop(0, TILES, first_stats, 0)
    for k in range(1, NCENT):
        remote(
            stat_send, stat_recv.at[cent], st_send.at[0], st_recv.at[0], at_cent((cent + k) % NCENT)
        ).start()
    stat_recv[cent] = stat_send[...]
    take(stat_recv.at[pl.ds(0, NCENT - 1)], st_recv.at[0])
    tops = [stat_recv[s, :, 0:4, :] for s in range(NCENT)]
    top = tops[0]
    for s in range(1, NCENT):
        top = jnp.maximum(top, tops[s])
    total = jnp.zeros_like(top)
    for s in range(NCENT):
        total += stat_recv[s, :, 4:8, :] * jnp.exp(tops[s] - top)
    factor[...] = jnp.exp(stat_send[:, 0:4, :] - top) / total

    norm_part[...] = jnp.zeros_like(norm_part)

    def responsibilities(t, carry):
        here = pl.ds(pl.multiple_of(t * LANES, LANES), LANES)
        value = (acc[:, here] * factor[t // 4, pl.ds(t % 4, 1), :]).astype(BF16)
        resp[:, here] = value
        norm_part[...] += value.astype(F32)
        return carry

    lax.fori_loop(0, TILES, responsibilities, 0)

    lane = lax.broadcasted_iota(jnp.int32, (NZ, OWN, LANES), 2)
    layer = lax.broadcasted_iota(jnp.int32, (NZ, OWN, LANES), 0)
    for i in range(NX):
        mass = jnp.sum(norm_part[i * NZ * OWN : (i + 1) * NZ * OWN, :], axis=1, keepdims=True)
        mass = jnp.broadcast_to(mass, (NZ * OWN, LANES)).reshape(NZ, OWN, LANES)
        count_send[i] = jnp.sum(jnp.where(lane == layer, mass, 0.0), axis=0)
    for k in (2, 1, 3):
        to = (x + k) % NX
        remote(
            count_send.at[to], count_recv.at[x], nx_send.at[0], nx_recv.at[0], at_zx(z, to)
        ).start()
    count_recv[x] = count_send[x]

    def sums_x(p):
        both = pl.ds(pl.multiple_of(2 * W * p, 2 * W), 2 * W)
        for i in range(NX):
            value = jnp.dot(
                resp[i * NZ * OWN : (i + 1) * NZ * OWN, :], rows[:, both], preferred_element_type=F32
            )
            left = value[:, :W].reshape(NZ, OWN, W)
            right = value[:, W:].reshape(NZ, OWN, W)
            packed = jnp.concatenate([left, right], axis=1)
            sums_f[p, i] = packed
            sums_send[p, i] = packed.astype(BF16)
        for k in (2, 1, 3):
            to = (x + k) % NX
            remote(
                sums_send.at[p, to], sums_recv.at[p, x], cx_send.at[p], cx_recv.at[p], at_zx(z, to)
            ).start()

    each_part(sums_x)

    take(count_recv.at[pl.ds(0, NX - 1)], nx_recv.at[0])
    total_send[...] = (count_recv[0] + count_recv[1]) + (count_recv[2] + count_recv[3])

    def send_total(step, carry):
        remote(
            total_send,
            total_recv.at[z],
            nz_send.at[0],
            nz_recv.at[0],
            at_zx((z + far_first(step)) % NZ, x),
        ).start()
        return carry

    lax.fori_loop(0, NZ - 1, send_total, 0)
    total_recv[z] = total_send[...]

    def sums_z(p):
        take(sums_recv.at[p, pl.ds(0, NX - 1)], cx_recv.at[p])
        value = sums_f[p, x]
        for k in range(1, NX):
            value += sums_recv[p, (x + k) % NX].astype(F32)
        part_send[p] = value.astype(BF16)

        def go(step, carry):
            to = (z + far_first(step)) % NZ
            remote(
                part_send.at[p, to], part_recv.at[p, z], cz_send.at[p], cz_recv.at[p], at_zx(to, x)
            ).start()
            return carry

        lax.fori_loop(0, NZ - 1, go, 0)
        part_recv[p, z] = part_send[p, z]

    each_part(sums_z)

    take(total_recv.at[pl.ds(0, NZ - 1)], nz_recv.at[0])
    mass = jnp.sum(total_recv[...], axis=0)
    own_lane = lax.broadcasted_iota(jnp.int32, (OWN, LANES), 1) == z
    mass = jnp.sum(jnp.where(own_lane, mass, 0.0), axis=1, keepdims=True) + prior_mass

    def renew(p):
        take(part_recv.at[p, pl.ds(0, NZ - 1)], cz_recv.at[p])
        value = jnp.sum(part_recv[p].astype(F32), axis=0)
        lo = pl.ds(pl.multiple_of(2 * W * p, 2 * W), W)
        hi = pl.ds(pl.multiple_of(2 * W * p + W, W), W)
        left = (value[:OWN] + prior_mass * cent_v[:, lo]) / mass
        right = (value[OWN:] + prior_mass * cent_v[:, hi]) / mass
        upd_out[:, lo] = left
        upd_out[:, hi] = right
        second[p, x, z] = jnp.concatenate([left, right], axis=0).astype(BF16)
        spread_z(second, p, uz_send, uz_recv)

    each_part(renew)
    each_part(lambda p: spread_x(second, p, ux_send, (uz_recv, ux_recv)))
    products(second, ux_recv)

    def second_stats(t, carry):
        here, score = score_tile(t)
        top = jnp.max(score, axis=0, keepdims=True)
        shifted = score - top
        weight = jnp.exp(shifted)
        stat2_send[t, 0:1, :] = top
        stat2_send[t, 1:2, :] = jnp.sum(weight, axis=0, keepdims=True)
        stat2_send[t, 2:3, :] = jnp.sum(weight * shifted, axis=0, keepdims=True)
        return carry

    lax.fori_loop(0, TILES, second_stats, 0)

    def chip_tiles(chip):
        return pl.ds(chip * CHIP_TILES, CHIP_TILES)

    for k in range(1, NCENT):
        to = (cent + k) % NCENT
        remote(
            stat2_send.at[chip_tiles(to // NC)],
            stat2_recv.at[cent],
            st2_send.at[0],
            st2_recv.at[0],
            at_cent(to),
        ).start()
    stat2_recv[cent] = stat2_send[chip_tiles(y)]
    take(stat2_recv.at[pl.ds(0, NCENT - 1)], st2_recv.at[0])
    tops = [stat2_recv[s, :, 0:1, :] for s in range(NCENT)]
    top = tops[0]
    for s in range(1, NCENT):
        top = jnp.maximum(top, tops[s])
    total = jnp.zeros_like(top)
    spread = jnp.zeros_like(top)
    for s in range(NCENT):
        gap = tops[s] - top
        scale = jnp.exp(gap)
        mine = stat2_recv[s, :, 1:2, :]
        total += scale * mine
        spread += scale * (stat2_recv[s, :, 2:3, :] + gap * mine)
    ent_out[...] = jnp.log(total) - spread / total

    for send in range(7):
        row_copy(cent, sibling, send).wait_send()
    take(stat_recv.at[pl.ds(0, NCENT - 1)], st_send.at[0])
    take(stat2_recv.at[pl.ds(0, NCENT - 1)], st2_send.at[0])
    take(count_recv.at[pl.ds(0, NX - 1)], nx_send.at[0])
    take(total_recv.at[pl.ds(0, NZ - 1)], nz_send.at[0])

    def drain(p):
        take(first.at[p, 0, pl.ds(0, NZ - 1)], gz_send.at[p])
        take(first.at[p, pl.ds(0, NX - 1)], gx_send.at[p])
        take(sums_recv.at[p, pl.ds(0, NX - 1)], cx_send.at[p])
        take(part_recv.at[p, pl.ds(0, NZ - 1)], cz_send.at[p])
        take(second.at[p, 0, pl.ds(0, NZ - 1)], uz_send.at[p])
        take(second.at[p, pl.ds(0, NX - 1)], ux_send.at[p])

    each_part(drain)


def on_device(embeddings, centroids):
    vmem = pltpu.VMEM
    dma = pltpu.SemaphoreType.DMA
    gathered = (PARTS, NX, NZ, 2 * OWN, W)
    updated, entropy = pl.pallas_call(
        kernel,
        out_shape=(
            jax.ShapeDtypeStruct((OWN, D), F32),
            jax.ShapeDtypeStruct((CHIP_TILES, 1, LANES), F32),
        ),
        in_specs=[pl.BlockSpec(memory_space=pl.ANY)] * 2,
        out_specs=(pl.BlockSpec(memory_space=vmem), pl.BlockSpec(memory_space=vmem)),
        scratch_shapes=[
            vmem((ROWS, D), F32),
            vmem((OWN, D), F32),
            vmem((GROUP, D), BF16),
            vmem(gathered, BF16),
            vmem(gathered, BF16),
            vmem((SLICE, D), BF16),
            vmem((SLICE, LANES), F32),
            vmem((SLICE, LANES), F32),
            vmem((1, GROUP), F32),
            vmem((SLICE, GROUP), F32),
            vmem((SLICE, GROUP), BF16),
            vmem((3, 8, LANES), F32),
            vmem((NCENT, 3, 8, LANES), F32),
            vmem((3, 4, LANES), F32),
            vmem((TILES, 8, LANES), F32),
            vmem((NCENT, CHIP_TILES, 8, LANES), F32),
            vmem(gathered, F32),
            vmem(gathered, BF16),
            vmem(gathered, BF16),
            vmem((PARTS, NZ, 2 * OWN, W), BF16),
            vmem((PARTS, NZ, 2 * OWN, W), BF16),
            vmem((NX, OWN, LANES), F32),
            vmem((NX, OWN, LANES), F32),
            vmem((OWN, LANES), F32),
            vmem((NZ, OWN, LANES), F32),
            dma((2,)),
            dma((7,)),
            dma((NCENT,)),
        ]
        + [dma((PARTS,))] * 4
        + [dma((1,))] * 2
        + [dma((PARTS,))] * 4
        + [dma((1,))] * 4
        + [dma((PARTS,))] * 4
        + [dma((1,))] * 2,
        compiler_params=pltpu.CompilerParams(
            collective_id=0, has_side_effects=True, vmem_limit_bytes=48 * 2**20
        ),
        name="em_update",
    )(embeddings, centroids)
    core = lax.axis_index("cent") % NC
    entropy = lax.dynamic_slice_in_dim(entropy.reshape(CHIP), core * ROWS, ROWS, 0)
    return updated, entropy


def solution(mesh):
    in_specs = (P(("dp", "cent"), None), P(("dp", "cent"), None))
    out_specs = (P(("dp", "cent"), None), P(("dp", "cent")))
    return jax.shard_map(
        on_device, mesh=mesh, in_specs=in_specs, out_specs=out_specs, check_vma=False
    )
```

```python
import jax
import jax.numpy as jnp
from jax import lax
from jax.experimental import pallas as pl
from jax.experimental.pallas import tpu as pltpu
from jax.sharding import PartitionSpec as P

MESH = pl.DeviceIdType.MESH
F32 = jnp.float32
BF16 = jnp.bfloat16

softness_level = 32.0
prior_mass = 4.0

D = 1024
NZ, NX, NY, NC = 16, 4, 4, 2
NCENT = NY * NC
ROWS = 192
GROUP = ROWS * NCENT
CHIP = ROWS * NC
OWN = 8
SLICE = OWN * NZ * NX
PARTS = 4
W = D // (2 * PARTS)
LANES = 128
TILES = GROUP // LANES
CHIP_TILES = CHIP // LANES
SCALE = 2.0 * softness_level
OFFSETS = (8, 7, 9, 6, 10, 5, 11, 4, 12, 3, 13, 2, 14, 1, 15, 0)
SLOT = {offset: slot for slot, offset in enumerate(OFFSETS)}
BACK = tuple(SLOT[(NZ - offset) % NZ] for offset in OFFSETS)
GROUPS = 4
PER = NZ // GROUPS
HOME = NZ - 1
HALF = ROWS // 2


def place():
    dp = lax.axis_index("dp")
    cent = lax.axis_index("cent")
    z = dp // NX
    x = dp % NX
    y = cent // NC
    core = cent % NC
    return z, x, y, core, cent


def kernel(
    emb_hbm,
    cent_hbm,
    upd_out,
    ent_out,
    emb_v,
    cent_v,
    rows,
    first,
    second,
    operand,
    norm_part,
    norm,
    row_sq,
    acc,
    resp,
    stat_send,
    stat_recv,
    factor,
    stat2_send,
    stat2_recv,
    sums_f,
    sums_send,
    sums_recv,
    part_send,
    part_recv,
    count_send,
    count_recv,
    total_send,
    total_recv,
    load_sem,
    rows_send_sem,
    rows_recv_sem,
    gz_send,
    gz_recv,
    gx_send,
    gx_recv,
    st_send,
    st_recv,
    cx_send,
    cx_recv,
    cz_send,
    cz_recv,
    nx_send,
    nx_recv,
    nz_send,
    nz_recv,
    uz_send,
    uz_recv,
    ux_send,
    ux_recv,
    st2_send,
    st2_recv,
):
    z, x, y, core, cent = place()

    def at_zx(z_to, x_to):
        return {"dp": z_to * NX + x_to, "cent": cent}

    def at_cent(cent_to):
        return {"dp": z * NX + x, "cent": cent_to}

    def remote(src, dst, send, recv, device):
        return pltpu.make_async_remote_copy(
            src_ref=src, dst_ref=dst, send_sem=send, recv_sem=recv, device_id=device, device_id_type=MESH
        )

    def take(ref, sem):
        pltpu.make_async_copy(ref, ref, sem).wait()

    pending = []

    def finish():
        for wait in pending:
            wait()

    def z_peer(slot):
        return lax.rem(z + OFFSETS[slot], NZ)

    barrier = pltpu.get_barrier_semaphore()
    for slot in range(HOME):
        pl.semaphore_signal(
            barrier, inc=1, device_id=at_zx(z_peer(slot), x), device_id_type=MESH
        )
    for k in range(1, NCENT):
        pl.semaphore_signal(
            barrier, inc=1, device_id=at_cent((cent + k) % NCENT), device_id_type=MESH
        )
    for k in range(1, NX):
        pl.semaphore_signal(barrier, inc=1, device_id=at_zx(z, (x + k) % NX), device_id_type=MESH)

    load_cent = pltpu.make_async_copy(cent_hbm, cent_v, load_sem.at[0])
    load_emb = pltpu.make_async_copy(emb_hbm, emb_v, load_sem.at[1])
    load_cent.start()
    load_emb.start()

    load_cent.wait()
    for p in range(PARTS):
        left = cent_v[:, 2 * W * p : 2 * W * p + W]
        right = cent_v[:, 2 * W * p + W : 2 * W * (p + 1)]
        first[p, x, HOME] = jnp.concatenate([left, right], axis=0).astype(BF16)
    load_emb.wait()
    own_rows = pl.ds(pl.multiple_of(cent * ROWS, ROWS), ROWS)
    rows[own_rows, :] = emb_v[...].astype(BF16)

    pl.semaphore_wait(barrier, (NZ - 1) + (NCENT - 1) + (NX - 1))

    def row_copy(owner, half, device, send):
        block = pl.ds(pl.multiple_of(owner * ROWS + half * HALF, HALF), HALF)
        return remote(
            rows.at[block, :],
            rows.at[block, :],
            rows_send_sem.at[send],
            rows_recv_sem.at[owner, half],
            device,
        )

    def owner_at(k):
        return lax.rem(y + k, NY) * NC + core

    up, down, far = owner_at(1), owner_at(3), owner_at(2)
    to_up, to_down, sibling = at_cent(up), at_cent(down), at_cent(y * NC + 1 - core)
    row_copy(cent, 0, to_up, 0).start()
    row_copy(cent, 1, to_down, 1).start()
    row_copy(cent, 1, to_up, 2).start()
    row_copy(cent, 0, to_down, 3).start()
    row_copy(cent, 0, sibling, 4).start()
    row_copy(cent, 1, sibling, 5).start()
    pending.append(lambda: [row_copy(cent, 0, sibling, k).wait_send() for k in range(14)])

    def spread_z(buf, p, send, recv):
        for slot in range(HOME):
            there = BACK[slot]
            remote(
                buf.at[p, x, HOME],
                buf.at[p, x, there],
                send.at[p],
                recv.at[p, there // PER],
                at_zx(z_peer(slot), x),
            ).start()

    def spread_x(buf, p, send, recv):
        for g in reversed(range(GROUPS)):
            count = PER - (g == GROUPS - 1)
            group = pl.ds(g * PER, PER)
            take(buf.at[p, x, pl.ds(g * PER, count)], recv[0].at[p, g])
            for k in (2, 1, 3):
                remote(
                    buf.at[p, x, group],
                    buf.at[p, x, group],
                    send.at[p],
                    recv[1].at[p],
                    at_zx(z, lax.rem(x + k, NX)),
                ).start()

    def each_part(body, start=0, stop=PARTS):
        def go(p, carry):
            body(p)
            return carry

        lax.fori_loop(start, stop, go, 0)

    each_part(lambda p: spread_z(first, p, gz_send, gz_recv))
    pending.append(lambda: each_part(lambda p: take(first.at[p, 0, pl.ds(0, NZ - 1)], gz_send.at[p])))

    spread_first = lambda p: spread_x(first, p, gx_send, (gz_recv, gx_recv))
    each_part(spread_first, 0, 1)
    row_copy(down, 0, sibling, 0).wait_recv()
    row_copy(down, 0, to_up, 6).start()
    row_copy(up, 1, sibling, 0).wait_recv()
    row_copy(up, 1, to_down, 7).start()
    row_copy(down, 0, sibling, 8).start()
    row_copy(up, 1, sibling, 9).start()
    each_part(spread_first, 1, 3)
    row_copy(down, 1, sibling, 0).wait_recv()
    row_copy(down, 1, sibling, 10).start()
    row_copy(up, 0, sibling, 0).wait_recv()
    row_copy(up, 0, sibling, 11).start()
    each_part(spread_first, 3, 4)
    pending.append(lambda: each_part(lambda p: take(first.at[p, pl.ds(0, NX - 1)], gx_send.at[p])))
    for half in range(2):
        row_copy(far, half, sibling, 0).wait_recv()
        row_copy(far, half, sibling, 12 + half).start()
    for k in range(NY):
        for half in range(2):
            row_copy(lax.rem(y + k, NY) * NC + 1 - core, half, sibling, 0).wait_recv()

    def row_norms(j, carry):
        here = pl.ds(pl.multiple_of(j * LANES, LANES), LANES)
        part = jnp.zeros((LANES, LANES), F32)
        for i in range(D // LANES):
            block = rows[here, i * LANES : (i + 1) * LANES].astype(F32)
            part += block * block
        row_sq[:, here] = jnp.sum(part.T, axis=0, keepdims=True)
        return carry

    lax.fori_loop(0, TILES, row_norms, 0)

    def products(buf, recv):
        def part(p):
            take(buf.at[p, pl.ds(0, NX - 1)], recv.at[p])
            lo = pl.ds(pl.multiple_of(2 * W * p, 2 * W), W)
            hi = pl.ds(pl.multiple_of(2 * W * p + W, W), W)
            both = pl.ds(pl.multiple_of(2 * W * p, 2 * W), 2 * W)
            for i in range(NX):
                block = buf[p, i].astype(F32)
                left = block[:, :OWN].reshape(NZ * OWN, W)
                right = block[:, OWN:].reshape(NZ * OWN, W)
                here = slice(i * NZ * OWN, (i + 1) * NZ * OWN)
                operand[here, lo] = left.astype(BF16)
                operand[here, hi] = right.astype(BF16)
                norm_part[here, :] += left * left + right * right
            acc[...] += lax.dot_general(
                operand[:, both],
                rows[:, both],
                (((1,), (1,)), ((), ())),
                preferred_element_type=F32,
            )

        each_part(part)
        norm[...] = jnp.broadcast_to(
            jnp.sum(norm_part[...], axis=1, keepdims=True), (SLICE, LANES)
        )

    def score_tile(t):
        here = slice(t * LANES, (t + 1) * LANES)
        return here, -(row_sq[:, here] - 2.0 * acc[:, here] + norm[...]) / SCALE

    norm_part[...] = jnp.zeros_like(norm_part)
    acc[...] = jnp.zeros_like(acc)
    products(first, gx_recv)

    for t in range(TILES):
        here, score = score_tile(t)
        top = jnp.max(score, axis=0, keepdims=True)
        weight = jnp.exp(score - top)
        acc[:, here] = weight
        stat_send[t // 4, t % 4 : t % 4 + 1, :] = top
        stat_send[t // 4, 4 + t % 4 : 5 + t % 4, :] = jnp.sum(weight, axis=0, keepdims=True)
    for k in range(1, NCENT):
        remote(
            stat_send, stat_recv.at[cent], st_send.at[0], st_recv.at[0], at_cent((cent + k) % NCENT)
        ).start()
    pending.append(lambda: take(stat_recv.at[pl.ds(0, NCENT - 1)], st_send.at[0]))
    stat_recv[cent] = stat_send[...]
    take(stat_recv.at[pl.ds(0, NCENT - 1)], st_recv.at[0])
    tops = [stat_recv[s, :, 0:4, :] for s in range(NCENT)]
    top = tops[0]
    for s in range(1, NCENT):
        top = jnp.maximum(top, tops[s])
    total = jnp.zeros_like(top)
    for s in range(NCENT):
        total += stat_recv[s, :, 4:8, :] * jnp.exp(tops[s] - top)
    factor[...] = jnp.exp(stat_send[:, 0:4, :] - top) / total

    for t in range(TILES):
        here = slice(t * LANES, (t + 1) * LANES)
        resp[:, here] = (acc[:, here] * factor[t // 4, t % 4 : t % 4 + 1, :]).astype(BF16)

    def sums_x(p):
        both = pl.ds(pl.multiple_of(2 * W * p, 2 * W), 2 * W)
        value = jnp.dot(resp[...], rows[:, both], preferred_element_type=F32)
        for i in range(NX):
            block = value[i * NZ * OWN : (i + 1) * NZ * OWN]
            left = block[:, :W].reshape(NZ, OWN, W)
            right = block[:, W:].reshape(NZ, OWN, W)
            packed = jnp.concatenate([left, right], axis=1)
            sums_f[p, i] = packed
            sums_send[p, i] = packed.astype(BF16)
        for g in range(GROUPS):
            group = pl.ds(g * PER, PER)
            for k in (2, 1, 3):
                to = lax.rem(x + k, NX)
                remote(
                    sums_send.at[p, to, group],
                    sums_recv.at[p, x, group],
                    cx_send.at[p],
                    cx_recv.at[p, g],
                    at_zx(z, to),
                ).start()

    each_part(sums_x, 0, 1)

    mass_part = jnp.zeros((SLICE, LANES), F32)
    for t in range(TILES):
        mass_part += resp[:, t * LANES : (t + 1) * LANES].astype(F32)
    norm_part[...] = mass_part
    lane = lax.broadcasted_iota(jnp.int32, (NZ, OWN, LANES), 2)
    layer = lax.broadcasted_iota(jnp.int32, (NZ, OWN, LANES), 0)
    for i in range(NX):
        mass = jnp.sum(norm_part[i * NZ * OWN : (i + 1) * NZ * OWN, :], axis=1, keepdims=True)
        mass = jnp.broadcast_to(mass, (NZ * OWN, LANES)).reshape(NZ, OWN, LANES)
        count_send[i] = jnp.sum(jnp.where(lane == layer, mass, 0.0), axis=0)
    for k in (2, 1, 3):
        to = lax.rem(x + k, NX)
        remote(
            count_send.at[to], count_recv.at[x], nx_send.at[0], nx_recv.at[0], at_zx(z, to)
        ).start()
    pending.append(lambda: take(count_recv.at[pl.ds(0, NX - 1)], nx_send.at[0]))
    count_recv[x] = count_send[x]

    each_part(sums_x, 1, PARTS)
    pending.append(lambda: each_part(lambda p: take(sums_recv.at[p, pl.ds(0, NX - 1)], cx_send.at[p])))

    def sums_z(p):
        for g in range(GROUPS):
            group = slice(g * PER, (g + 1) * PER)
            take(sums_recv.at[p, pl.ds(0, NX - 1), pl.ds(g * PER, PER)], cx_recv.at[p, g])
            value = sums_f[p, x, group]
            for k in range(1, NX):
                value += sums_recv[p, lax.rem(x + k, NX), group].astype(F32)
            part_send[p, group] = value.astype(BF16)
            for slot in range(g * PER, (g + 1) * PER):
                if slot != HOME:
                    remote(
                        part_send.at[p, slot],
                        part_recv.at[p, BACK[slot]],
                        cz_send.at[p],
                        cz_recv.at[p],
                        at_zx(z_peer(slot), x),
                    ).start()
        part_recv[p, HOME] = part_send[p, HOME]

    each_part(sums_z, 0, 2)

    take(count_recv.at[pl.ds(0, NX - 1)], nx_recv.at[0])
    total_send[...] = (count_recv[0] + count_recv[1]) + (count_recv[2] + count_recv[3])
    for slot in range(HOME):
        remote(
            total_send,
            total_recv.at[BACK[slot]],
            nz_send.at[0],
            nz_recv.at[0],
            at_zx(z_peer(slot), x),
        ).start()
    pending.append(lambda: take(total_recv.at[pl.ds(0, NZ - 1)], nz_send.at[0]))
    total_recv[HOME] = total_send[...]

    each_part(sums_z, 2, PARTS)
    pending.append(lambda: each_part(lambda p: take(part_recv.at[p, pl.ds(0, NZ - 1)], cz_send.at[p])))

    norm_part[...] = jnp.zeros_like(norm_part)
    acc[...] = jnp.zeros_like(acc)

    take(total_recv.at[pl.ds(0, NZ - 1)], nz_recv.at[0])
    lane = lax.broadcasted_iota(jnp.int32, (OWN, LANES), 1)
    mass = jnp.zeros((OWN, LANES), F32)
    for slot in range(NZ):
        mass += jnp.where(lane == BACK[slot], total_recv[slot], 0.0)
    mass = jnp.sum(mass, axis=1, keepdims=True) + prior_mass

    def renew(p):
        take(part_recv.at[p, pl.ds(0, NZ - 1)], cz_recv.at[p])
        value = jnp.sum(part_recv[p].astype(F32), axis=0)
        lo = pl.ds(pl.multiple_of(2 * W * p, 2 * W), W)
        hi = pl.ds(pl.multiple_of(2 * W * p + W, W), W)
        left = (value[:OWN] + prior_mass * cent_v[:, lo]) / mass
        right = (value[OWN:] + prior_mass * cent_v[:, hi]) / mass
        upd_out[:, lo] = left
        upd_out[:, hi] = right
        second[p, x, HOME] = jnp.concatenate([left, right], axis=0).astype(BF16)
        spread_z(second, p, uz_send, uz_recv)

    each_part(renew)
    pending.append(lambda: each_part(lambda p: take(second.at[p, 0, pl.ds(0, NZ - 1)], uz_send.at[p])))
    each_part(lambda p: spread_x(second, p, ux_send, (uz_recv, ux_recv)))
    pending.append(lambda: each_part(lambda p: take(second.at[p, pl.ds(0, NX - 1)], ux_send.at[p])))
    products(second, ux_recv)

    for t in range(TILES):
        here, score = score_tile(t)
        top = jnp.max(score, axis=0, keepdims=True)
        shifted = score - top
        weight = jnp.exp(shifted)
        stat2_send[t, 0:1, :] = top
        stat2_send[t, 1:2, :] = jnp.sum(weight, axis=0, keepdims=True)
        stat2_send[t, 2:3, :] = jnp.sum(weight * shifted, axis=0, keepdims=True)

    def chip_tiles(chip):
        return pl.ds(chip * CHIP_TILES, CHIP_TILES)

    for k in range(1, NCENT):
        to = (cent + k) % NCENT
        remote(
            stat2_send.at[chip_tiles(to // NC)],
            stat2_recv.at[cent],
            st2_send.at[0],
            st2_recv.at[0],
            at_cent(to),
        ).start()
    pending.append(lambda: take(stat2_recv.at[pl.ds(0, NCENT - 1)], st2_send.at[0]))
    stat2_recv[cent] = stat2_send[chip_tiles(y)]
    take(stat2_recv.at[pl.ds(0, NCENT - 1)], st2_recv.at[0])
    tops = [stat2_recv[s, :, 0:1, :] for s in range(NCENT)]
    top = tops[0]
    for s in range(1, NCENT):
        top = jnp.maximum(top, tops[s])
    total = jnp.zeros_like(top)
    spread = jnp.zeros_like(top)
    for s in range(NCENT):
        gap = tops[s] - top
        scale = jnp.exp(gap)
        mine = stat2_recv[s, :, 1:2, :]
        total += scale * mine
        spread += scale * (stat2_recv[s, :, 2:3, :] + gap * mine)
    ent_out[...] = jnp.log(total) - spread / total

    finish()


def on_device(embeddings, centroids):
    vmem = pltpu.VMEM
    dma = pltpu.SemaphoreType.DMA
    gathered = (PARTS, NX, NZ, 2 * OWN, W)
    updated, entropy = pl.pallas_call(
        kernel,
        out_shape=(
            jax.ShapeDtypeStruct((OWN, D), F32),
            jax.ShapeDtypeStruct((CHIP_TILES, 1, LANES), F32),
        ),
        in_specs=[pl.BlockSpec(memory_space=pl.ANY)] * 2,
        out_specs=(pl.BlockSpec(memory_space=vmem), pl.BlockSpec(memory_space=vmem)),
        scratch_shapes=[
            vmem((ROWS, D), F32),
            vmem((OWN, D), F32),
            vmem((GROUP, D), BF16),
            vmem(gathered, BF16),
            vmem(gathered, BF16),
            vmem((SLICE, D), BF16),
            vmem((SLICE, LANES), F32),
            vmem((SLICE, LANES), F32),
            vmem((1, GROUP), F32),
            vmem((SLICE, GROUP), F32),
            vmem((SLICE, GROUP), BF16),
            vmem((3, 8, LANES), F32),
            vmem((NCENT, 3, 8, LANES), F32),
            vmem((3, 4, LANES), F32),
            vmem((TILES, 8, LANES), F32),
            vmem((NCENT, CHIP_TILES, 8, LANES), F32),
            vmem(gathered, F32),
            vmem(gathered, BF16),
            vmem(gathered, BF16),
            vmem((PARTS, NZ, 2 * OWN, W), BF16),
            vmem((PARTS, NZ, 2 * OWN, W), BF16),
            vmem((NX, OWN, LANES), F32),
            vmem((NX, OWN, LANES), F32),
            vmem((OWN, LANES), F32),
            vmem((NZ, OWN, LANES), F32),
            dma((2,)),
            dma((14,)),
            dma((NCENT, 2)),
            dma((PARTS,)),
            dma((PARTS, GROUPS)),
            dma((PARTS,)),
            dma((PARTS,)),
            dma((1,)),
            dma((1,)),
            dma((PARTS,)),
            dma((PARTS, GROUPS)),
            dma((PARTS,)),
            dma((PARTS,)),
            dma((1,)),
            dma((1,)),
            dma((1,)),
            dma((1,)),
            dma((PARTS,)),
            dma((PARTS, GROUPS)),
            dma((PARTS,)),
            dma((PARTS,)),
            dma((1,)),
            dma((1,)),
        ],
        compiler_params=pltpu.CompilerParams(
            collective_id=0, has_side_effects=True, vmem_limit_bytes=63 * 2**20
        ),
        name="em_update",
    )(embeddings, centroids)
    core = lax.axis_index("cent") % NC
    entropy = lax.dynamic_slice_in_dim(entropy.reshape(CHIP), core * ROWS, ROWS, 0)
    return updated, entropy


def solution(mesh):
    in_specs = (P(("dp", "cent"), None), P(("dp", "cent"), None))
    out_specs = (P(("dp", "cent"), None), P(("dp", "cent")))
    return jax.shard_map(
        on_device, mesh=mesh, in_specs=in_specs, out_specs=out_specs, check_vma=False
    )
```

```python
import jax
import jax.numpy as jnp
from jax import lax
from jax.experimental import pallas as pl
from jax.experimental.pallas import tpu as pltpu
from jax.sharding import PartitionSpec as P

MESH = pl.DeviceIdType.MESH
F32 = jnp.float32
BF16 = jnp.bfloat16

softness_level = 32.0
prior_mass = 4.0

D = 1024
NZ, NX, NY, NC = 16, 4, 4, 2
NCENT = NY * NC
ROWS = 192
GROUP = ROWS * NCENT
CHIP = ROWS * NC
OWN = 8
SLICE = OWN * NZ * NX
PARTS = 4
W = D // (2 * PARTS)
LANES = 128
TILES = GROUP // LANES
CHIP_TILES = CHIP // LANES
SCALE = 2.0 * softness_level
OFFSETS = (8, 7, 9, 6, 10, 5, 11, 4, 12, 3, 13, 2, 14, 1, 15, 0)
SLOT = {offset: slot for slot, offset in enumerate(OFFSETS)}
BACK = tuple(SLOT[(NZ - offset) % NZ] for offset in OFFSETS)
GROUPS = 4
PER = NZ // GROUPS
HOME = NZ - 1
HALF = ROWS // 2


def place():
    dp = lax.axis_index("dp")
    cent = lax.axis_index("cent")
    z = dp // NX
    x = dp % NX
    y = cent // NC
    core = cent % NC
    return z, x, y, core, cent


def kernel(
    emb_hbm,
    cent_hbm,
    upd_out,
    ent_out,
    emb_v,
    cent_v,
    rows,
    first,
    second,
    operand,
    norm_part,
    norm,
    row_sq,
    acc,
    resp,
    stat_send,
    stat_recv,
    factor,
    stat2_send,
    stat2_recv,
    sums_f,
    sums_send,
    sums_recv,
    part_send,
    part_recv,
    count_send,
    count_recv,
    total_send,
    total_recv,
    load_sem,
    rows_send_sem,
    rows_recv_sem,
    gz_send,
    gz_recv,
    gx_send,
    gx_recv,
    st_send,
    st_recv,
    cx_send,
    cx_recv,
    cz_send,
    cz_recv,
    nx_send,
    nx_recv,
    nz_send,
    nz_recv,
    uz_send,
    uz_recv,
    ux_send,
    ux_recv,
    st2_send,
    st2_recv,
):
    z, x, y, core, cent = place()

    def at_zx(z_to, x_to):
        return {"dp": z_to * NX + x_to, "cent": cent}

    def at_cent(cent_to):
        return {"dp": z * NX + x, "cent": cent_to}

    def remote(src, dst, send, recv, device):
        return pltpu.make_async_remote_copy(
            src_ref=src, dst_ref=dst, send_sem=send, recv_sem=recv, device_id=device, device_id_type=MESH
        )

    def take(ref, sem):
        pltpu.make_async_copy(ref, ref, sem).wait()

    pending = []

    def finish():
        for wait in pending:
            wait()

    def z_peer(slot):
        return lax.rem(z + OFFSETS[slot], NZ)

    barrier = pltpu.get_barrier_semaphore()
    for slot in range(HOME):
        pl.semaphore_signal(
            barrier, inc=1, device_id=at_zx(z_peer(slot), x), device_id_type=MESH
        )
    for k in range(1, NCENT):
        pl.semaphore_signal(
            barrier, inc=1, device_id=at_cent((cent + k) % NCENT), device_id_type=MESH
        )
    for k in range(1, NX):
        pl.semaphore_signal(barrier, inc=1, device_id=at_zx(z, (x + k) % NX), device_id_type=MESH)

    load_cent = pltpu.make_async_copy(cent_hbm, cent_v, load_sem.at[0])
    load_emb = pltpu.make_async_copy(emb_hbm, emb_v, load_sem.at[1])
    load_cent.start()
    load_emb.start()

    load_cent.wait()
    for p in range(PARTS):
        left = cent_v[:, 2 * W * p : 2 * W * p + W]
        right = cent_v[:, 2 * W * p + W : 2 * W * (p + 1)]
        first[p, x, HOME] = jnp.concatenate([left, right], axis=0).astype(BF16)
    load_emb.wait()
    own_rows = pl.ds(pl.multiple_of(cent * ROWS, ROWS), ROWS)
    rows[own_rows, :] = emb_v[...].astype(BF16)

    pl.semaphore_wait(barrier, (NZ - 1) + (NCENT - 1) + (NX - 1))

    def row_copy(owner, half, device, send):
        block = pl.ds(pl.multiple_of(owner * ROWS + half * HALF, HALF), HALF)
        return remote(
            rows.at[block, :],
            rows.at[block, :],
            rows_send_sem.at[send],
            rows_recv_sem.at[owner, half],
            device,
        )

    def owner_at(k):
        return lax.rem(y + k, NY) * NC + core

    up, down, far = owner_at(1), owner_at(3), owner_at(2)
    to_up, to_down, sibling = at_cent(up), at_cent(down), at_cent(y * NC + 1 - core)
    row_copy(cent, 0, to_up, 0).start()
    row_copy(cent, 1, to_down, 1).start()
    row_copy(cent, 0, sibling, 4).start()
    row_copy(cent, 1, sibling, 5).start()
    pending.append(lambda: [row_copy(cent, 0, sibling, k).wait_send() for k in range(2, 14)])

    def spread_z(buf, p, send, recv):
        for slot in range(HOME):
            there = BACK[slot]
            remote(
                buf.at[p, x, HOME],
                buf.at[p, x, there],
                send.at[p],
                recv.at[p, there // PER],
                at_zx(z_peer(slot), x),
            ).start()

    def spread_x(buf, p, g, send, recv):
        group = pl.ds(g * PER, PER)
        take(buf.at[p, x, pl.ds(g * PER, PER - (g == GROUPS - 1))], recv[0].at[p, g])
        for k in (2, 1, 3):
            remote(
                buf.at[p, x, group],
                buf.at[p, x, group],
                send.at[p],
                recv[1].at[p],
                at_zx(z, lax.rem(x + k, NX)),
            ).start()

    def in_order(lag):
        pieces = [(p, g) for p in range(PARTS) for g in range(GROUPS)]
        return sorted(pieces, key=lambda piece: piece[0] + lag * (GROUPS - 1 - piece[1]))

    def each_part(body, start=0, stop=PARTS):
        def go(p, carry):
            body(p)
            return carry

        lax.fori_loop(start, stop, go, 0)

    each_part(lambda p: spread_z(first, p, gz_send, gz_recv))
    pending.append(lambda: each_part(lambda p: take(first.at[p, 0, pl.ds(0, NZ - 1)], gz_send.at[p])))

    row_copy(cent, 0, to_up, 0).wait_send()
    row_copy(cent, 1, to_up, 2).start()
    row_copy(cent, 1, to_down, 1).wait_send()
    row_copy(cent, 0, to_down, 3).start()

    steps = in_order(0.6)

    def spread_first(start, stop):
        for p, g in steps[start:stop]:
            spread_x(first, p, g, gx_send, (gz_recv, gx_recv))

    def chip_norms(k):
        chip = lax.rem(y + k, NY)
        for half in range(2):
            row_copy(chip * NC + 1 - core, half, sibling, 0).wait_recv()
        for j in range(CHIP_TILES):
            here = pl.ds(pl.multiple_of(chip * CHIP + j * LANES, LANES), LANES)
            part = jnp.zeros((LANES, LANES), F32)
            for i in range(D // LANES):
                block = rows[here, i * LANES : (i + 1) * LANES].astype(F32)
                part += block * block
            row_sq[:, here] = jnp.sum(part.T, axis=0, keepdims=True)

    spread_first(0, 2)
    row_copy(down, 0, sibling, 0).wait_recv()
    row_copy(down, 0, to_up, 6).start()
    row_copy(up, 1, sibling, 0).wait_recv()
    row_copy(up, 1, to_down, 7).start()
    row_copy(down, 0, sibling, 8).start()
    row_copy(up, 1, sibling, 9).start()
    spread_first(2, 8)
    row_copy(down, 1, sibling, 0).wait_recv()
    row_copy(down, 1, sibling, 10).start()
    row_copy(up, 0, sibling, 0).wait_recv()
    row_copy(up, 0, sibling, 11).start()
    spread_first(8, 12)
    norm_part[...] = jnp.zeros_like(norm_part)
    acc[...] = jnp.zeros_like(acc)
    chip_norms(0)
    spread_first(12, 16)
    pending.append(lambda: each_part(lambda p: take(first.at[p, pl.ds(0, NX - 1)], gx_send.at[p])))
    chip_norms(1)
    chip_norms(3)
    for half in range(2):
        row_copy(far, half, sibling, 0).wait_recv()
        row_copy(far, half, sibling, 12 + half).start()
    chip_norms(2)

    def products(buf, recv):
        def part(p):
            take(buf.at[p, pl.ds(0, NX - 1)], recv.at[p])
            lo = pl.ds(pl.multiple_of(2 * W * p, 2 * W), W)
            hi = pl.ds(pl.multiple_of(2 * W * p + W, W), W)
            both = pl.ds(pl.multiple_of(2 * W * p, 2 * W), 2 * W)
            for i in range(NX):
                block = buf[p, i].astype(F32)
                left = block[:, :OWN].reshape(NZ * OWN, W)
                right = block[:, OWN:].reshape(NZ * OWN, W)
                here = slice(i * NZ * OWN, (i + 1) * NZ * OWN)
                operand[here, lo] = left.astype(BF16)
                operand[here, hi] = right.astype(BF16)
                norm_part[here, :] += left * left + right * right
            acc[...] += lax.dot_general(
                operand[:, both],
                rows[:, both],
                (((1,), (1,)), ((), ())),
                preferred_element_type=F32,
            )

        each_part(part)
        norm[...] = jnp.broadcast_to(
            jnp.sum(norm_part[...], axis=1, keepdims=True), (SLICE, LANES)
        )

    def score_tile(t):
        here = slice(t * LANES, (t + 1) * LANES)
        return here, -(row_sq[:, here] - 2.0 * acc[:, here] + norm[...]) / SCALE

    products(first, gx_recv)

    for t in range(TILES):
        here, score = score_tile(t)
        top = jnp.max(score, axis=0, keepdims=True)
        weight = jnp.exp(score - top)
        acc[:, here] = weight
        stat_send[t // 4, t % 4 : t % 4 + 1, :] = top
        stat_send[t // 4, 4 + t % 4 : 5 + t % 4, :] = jnp.sum(weight, axis=0, keepdims=True)
    for k in range(1, NCENT):
        remote(
            stat_send, stat_recv.at[cent], st_send.at[0], st_recv.at[0], at_cent((cent + k) % NCENT)
        ).start()
    pending.append(lambda: take(stat_recv.at[pl.ds(0, NCENT - 1)], st_send.at[0]))
    stat_recv[cent] = stat_send[...]
    take(stat_recv.at[pl.ds(0, NCENT - 1)], st_recv.at[0])
    tops = [stat_recv[s, :, 0:4, :] for s in range(NCENT)]
    top = tops[0]
    for s in range(1, NCENT):
        top = jnp.maximum(top, tops[s])
    total = jnp.zeros_like(top)
    for s in range(NCENT):
        total += stat_recv[s, :, 4:8, :] * jnp.exp(tops[s] - top)
    factor[...] = jnp.exp(stat_send[:, 0:4, :] - top) / total

    for t in range(TILES):
        here = slice(t * LANES, (t + 1) * LANES)
        resp[:, here] = (acc[:, here] * factor[t // 4, t % 4 : t % 4 + 1, :]).astype(BF16)

    def sums_x(p):
        both = pl.ds(pl.multiple_of(2 * W * p, 2 * W), 2 * W)
        value = jnp.dot(resp[...], rows[:, both], preferred_element_type=F32)
        for i in range(NX):
            block = value[i * NZ * OWN : (i + 1) * NZ * OWN]
            left = block[:, :W].reshape(NZ, OWN, W)
            right = block[:, W:].reshape(NZ, OWN, W)
            packed = jnp.concatenate([left, right], axis=1)
            sums_f[p, i] = packed
            sums_send[p, i] = packed.astype(BF16)
        for g in range(GROUPS):
            group = pl.ds(g * PER, PER)
            for k in (2, 1, 3):
                to = lax.rem(x + k, NX)
                remote(
                    sums_send.at[p, to, group],
                    sums_recv.at[p, x, group],
                    cx_send.at[p],
                    cx_recv.at[p, g],
                    at_zx(z, to),
                ).start()

    each_part(sums_x, 0, 1)

    mass_part = jnp.zeros((SLICE, LANES), F32)
    for t in range(TILES):
        mass_part += resp[:, t * LANES : (t + 1) * LANES].astype(F32)
    norm_part[...] = mass_part
    lane = lax.broadcasted_iota(jnp.int32, (NZ, OWN, LANES), 2)
    layer = lax.broadcasted_iota(jnp.int32, (NZ, OWN, LANES), 0)
    for i in range(NX):
        mass = jnp.sum(norm_part[i * NZ * OWN : (i + 1) * NZ * OWN, :], axis=1, keepdims=True)
        mass = jnp.broadcast_to(mass, (NZ * OWN, LANES)).reshape(NZ, OWN, LANES)
        count_send[i] = jnp.sum(jnp.where(lane == layer, mass, 0.0), axis=0)
    for k in (2, 1, 3):
        to = lax.rem(x + k, NX)
        remote(
            count_send.at[to], count_recv.at[x], nx_send.at[0], nx_recv.at[0], at_zx(z, to)
        ).start()
    pending.append(lambda: take(count_recv.at[pl.ds(0, NX - 1)], nx_send.at[0]))
    count_recv[x] = count_send[x]

    each_part(sums_x, 1, PARTS)
    pending.append(lambda: each_part(lambda p: take(sums_recv.at[p, pl.ds(0, NX - 1)], cx_send.at[p])))

    def sums_z(p):
        for g in range(GROUPS):
            group = slice(g * PER, (g + 1) * PER)
            take(sums_recv.at[p, pl.ds(0, NX - 1), pl.ds(g * PER, PER)], cx_recv.at[p, g])
            value = sums_f[p, x, group]
            for k in range(1, NX):
                value += sums_recv[p, lax.rem(x + k, NX), group].astype(F32)
            part_send[p, group] = value.astype(BF16)
            for slot in range(g * PER, (g + 1) * PER):
                if slot != HOME:
                    remote(
                        part_send.at[p, slot],
                        part_recv.at[p, BACK[slot]],
                        cz_send.at[p],
                        cz_recv.at[p],
                        at_zx(z_peer(slot), x),
                    ).start()
        part_recv[p, HOME] = part_send[p, HOME]

    each_part(sums_z, 0, 2)

    take(count_recv.at[pl.ds(0, NX - 1)], nx_recv.at[0])
    total_send[...] = (count_recv[0] + count_recv[1]) + (count_recv[2] + count_recv[3])
    for slot in range(HOME):
        remote(
            total_send,
            total_recv.at[BACK[slot]],
            nz_send.at[0],
            nz_recv.at[0],
            at_zx(z_peer(slot), x),
        ).start()
    pending.append(lambda: take(total_recv.at[pl.ds(0, NZ - 1)], nz_send.at[0]))
    total_recv[HOME] = total_send[...]

    each_part(sums_z, 2, PARTS)
    pending.append(lambda: each_part(lambda p: take(part_recv.at[p, pl.ds(0, NZ - 1)], cz_send.at[p])))

    norm_part[...] = jnp.zeros_like(norm_part)
    acc[...] = jnp.zeros_like(acc)

    take(total_recv.at[pl.ds(0, NZ - 1)], nz_recv.at[0])
    lane = lax.broadcasted_iota(jnp.int32, (OWN, LANES), 1)
    mass = jnp.zeros((OWN, LANES), F32)
    for slot in range(NZ):
        mass += jnp.where(lane == BACK[slot], total_recv[slot], 0.0)
    mass = jnp.sum(mass, axis=1, keepdims=True) + prior_mass

    def renew(p):
        take(part_recv.at[p, pl.ds(0, NZ - 1)], cz_recv.at[p])
        value = jnp.sum(part_recv[p].astype(F32), axis=0)
        lo = pl.ds(pl.multiple_of(2 * W * p, 2 * W), W)
        hi = pl.ds(pl.multiple_of(2 * W * p + W, W), W)
        left = (value[:OWN] + prior_mass * cent_v[:, lo]) / mass
        right = (value[OWN:] + prior_mass * cent_v[:, hi]) / mass
        upd_out[:, lo] = left
        upd_out[:, hi] = right
        second[p, x, HOME] = jnp.concatenate([left, right], axis=0).astype(BF16)
        spread_z(second, p, uz_send, uz_recv)

    renew(0)
    renew(1)
    done = 1
    for p, g in in_order(0.9):
        if done < min(p + 1 + (GROUPS - 1 - g) // 2, PARTS - 1) or done < p:
            done += 1
            renew(done)
        spread_x(second, p, g, ux_send, (uz_recv, ux_recv))
    pending.append(lambda: each_part(lambda p: take(second.at[p, 0, pl.ds(0, NZ - 1)], uz_send.at[p])))
    pending.append(lambda: each_part(lambda p: take(second.at[p, pl.ds(0, NX - 1)], ux_send.at[p])))
    products(second, ux_recv)

    for t in range(TILES):
        here, score = score_tile(t)
        top = jnp.max(score, axis=0, keepdims=True)
        shifted = score - top
        weight = jnp.exp(shifted)
        stat2_send[t, 0:1, :] = top
        stat2_send[t, 1:2, :] = jnp.sum(weight, axis=0, keepdims=True)
        stat2_send[t, 2:3, :] = jnp.sum(weight * shifted, axis=0, keepdims=True)

    def chip_tiles(chip):
        return pl.ds(chip * CHIP_TILES, CHIP_TILES)

    for k in range(1, NCENT):
        to = (cent + k) % NCENT
        remote(
            stat2_send.at[chip_tiles(to // NC)],
            stat2_recv.at[cent],
            st2_send.at[0],
            st2_recv.at[0],
            at_cent(to),
        ).start()
    pending.append(lambda: take(stat2_recv.at[pl.ds(0, NCENT - 1)], st2_send.at[0]))
    stat2_recv[cent] = stat2_send[chip_tiles(y)]
    finish()
    take(stat2_recv.at[pl.ds(0, NCENT - 1)], st2_recv.at[0])
    tops = [stat2_recv[s, :, 0:1, :] for s in range(NCENT)]
    top = tops[0]
    for s in range(1, NCENT):
        top = jnp.maximum(top, tops[s])
    total = jnp.zeros_like(top)
    spread = jnp.zeros_like(top)
    for s in range(NCENT):
        gap = tops[s] - top
        scale = jnp.exp(gap)
        mine = stat2_recv[s, :, 1:2, :]
        total += scale * mine
        spread += scale * (stat2_recv[s, :, 2:3, :] + gap * mine)
    ent_out[...] = jnp.log(total) - spread / total


def on_device(embeddings, centroids):
    vmem = pltpu.VMEM
    dma = pltpu.SemaphoreType.DMA
    gathered = (PARTS, NX, NZ, 2 * OWN, W)
    updated, entropy = pl.pallas_call(
        kernel,
        out_shape=(
            jax.ShapeDtypeStruct((OWN, D), F32),
            jax.ShapeDtypeStruct((CHIP_TILES, 1, LANES), F32),
        ),
        in_specs=[pl.BlockSpec(memory_space=pl.ANY)] * 2,
        out_specs=(pl.BlockSpec(memory_space=vmem), pl.BlockSpec(memory_space=vmem)),
        scratch_shapes=[
            vmem((ROWS, D), F32),
            vmem((OWN, D), F32),
            vmem((GROUP, D), BF16),
            vmem(gathered, BF16),
            vmem(gathered, BF16),
            vmem((SLICE, D), BF16),
            vmem((SLICE, LANES), F32),
            vmem((SLICE, LANES), F32),
            vmem((1, GROUP), F32),
            vmem((SLICE, GROUP), F32),
            vmem((SLICE, GROUP), BF16),
            vmem((3, 8, LANES), F32),
            vmem((NCENT, 3, 8, LANES), F32),
            vmem((3, 4, LANES), F32),
            vmem((TILES, 8, LANES), F32),
            vmem((NCENT, CHIP_TILES, 8, LANES), F32),
            vmem(gathered, F32),
            vmem(gathered, BF16),
            vmem(gathered, BF16),
            vmem((PARTS, NZ, 2 * OWN, W), BF16),
            vmem((PARTS, NZ, 2 * OWN, W), BF16),
            vmem((NX, OWN, LANES), F32),
            vmem((NX, OWN, LANES), F32),
            vmem((OWN, LANES), F32),
            vmem((NZ, OWN, LANES), F32),
            dma((2,)),
            dma((14,)),
            dma((NCENT, 2)),
            dma((PARTS,)),
            dma((PARTS, GROUPS)),
            dma((PARTS,)),
            dma((PARTS,)),
            dma((1,)),
            dma((1,)),
            dma((PARTS,)),
            dma((PARTS, GROUPS)),
            dma((PARTS,)),
            dma((PARTS,)),
            dma((1,)),
            dma((1,)),
            dma((1,)),
            dma((1,)),
            dma((PARTS,)),
            dma((PARTS, GROUPS)),
            dma((PARTS,)),
            dma((PARTS,)),
            dma((1,)),
            dma((1,)),
        ],
        compiler_params=pltpu.CompilerParams(
            collective_id=0, has_side_effects=True, vmem_limit_bytes=63 * 2**20
        ),
        name="em_update",
    )(embeddings, centroids)
    core = lax.axis_index("cent") % NC
    entropy = lax.dynamic_slice_in_dim(entropy.reshape(CHIP), core * ROWS, ROWS, 0)
    return updated, entropy


def solution(mesh):
    in_specs = (P(("dp", "cent"), None), P(("dp", "cent"), None))
    out_specs = (P(("dp", "cent"), None), P(("dp", "cent")))
    return jax.shard_map(
        on_device, mesh=mesh, in_specs=in_specs, out_specs=out_specs, check_vma=False
    )
```

```python
import jax
import jax.numpy as jnp
from jax import lax
from jax.experimental import pallas as pl
from jax.experimental.pallas import tpu as pltpu
from jax.sharding import PartitionSpec as P

MESH = pl.DeviceIdType.MESH
F32 = jnp.float32
BF16 = jnp.bfloat16

softness_level = 32.0
prior_mass = 4.0

D = 1024
NZ, NX, NY, NC = 16, 4, 4, 2
NCENT = NY * NC
ROWS = 192
GROUP = ROWS * NCENT
CHIP = ROWS * NC
OWN = 8
SLICE = OWN * NZ * NX
PARTS = 4
W = D // (2 * PARTS)
LANES = 128
TILES = GROUP // LANES
CHIP_TILES = CHIP // LANES
SCALE = 2.0 * softness_level
OFFSETS = (8, 7, 9, 6, 10, 5, 11, 4, 12, 3, 13, 2, 14, 1, 15, 0)
SLOT = {offset: slot for slot, offset in enumerate(OFFSETS)}
BACK = tuple(SLOT[(NZ - offset) % NZ] for offset in OFFSETS)
GROUPS = 4
PER = NZ // GROUPS
HOME = NZ - 1
HALF = ROWS // 2


def place():
    dp = lax.axis_index("dp")
    cent = lax.axis_index("cent")
    z = dp // NX
    x = dp % NX
    y = cent // NC
    core = cent % NC
    return z, x, y, core, cent


def kernel(
    emb_hbm,
    cent_hbm,
    upd_out,
    ent_out,
    emb_v,
    cent_v,
    rows,
    first,
    second,
    operand,
    norm_part,
    norm,
    row_sq,
    acc,
    resp,
    stat_send,
    stat_recv,
    factor,
    stat2_send,
    stat2_recv,
    sums_f,
    sums_send,
    sums_recv,
    part_send,
    part_recv,
    count_send,
    count_recv,
    total_send,
    total_recv,
    load_sem,
    rows_send_sem,
    rows_recv_sem,
    gz_send,
    gz_recv,
    gx_send,
    gx_recv,
    st_send,
    st_recv,
    cx_send,
    cx_recv,
    cz_send,
    cz_recv,
    nx_send,
    nx_recv,
    nz_send,
    nz_recv,
    uz_send,
    uz_recv,
    ux_send,
    ux_recv,
    st2_send,
    st2_recv,
):
    z, x, y, core, cent = place()

    def at_zx(z_to, x_to):
        return {"dp": z_to * NX + x_to, "cent": cent}

    def at_cent(cent_to):
        return {"dp": z * NX + x, "cent": cent_to}

    def remote(src, dst, send, recv, device):
        return pltpu.make_async_remote_copy(
            src_ref=src, dst_ref=dst, send_sem=send, recv_sem=recv, device_id=device, device_id_type=MESH
        )

    def take(ref, sem):
        pltpu.make_async_copy(ref, ref, sem).wait()

    pending = []

    def finish():
        for wait in pending:
            wait()

    def z_peer(slot):
        return lax.rem(z + OFFSETS[slot], NZ)

    barrier = pltpu.get_barrier_semaphore()
    for slot in range(HOME):
        pl.semaphore_signal(
            barrier, inc=1, device_id=at_zx(z_peer(slot), x), device_id_type=MESH
        )
    for k in range(1, NCENT):
        pl.semaphore_signal(
            barrier, inc=1, device_id=at_cent((cent + k) % NCENT), device_id_type=MESH
        )
    for k in range(1, NX):
        pl.semaphore_signal(barrier, inc=1, device_id=at_zx(z, (x + k) % NX), device_id_type=MESH)

    load_cent = pltpu.make_async_copy(cent_hbm, cent_v, load_sem.at[0])
    load_emb = pltpu.make_async_copy(emb_hbm, emb_v, load_sem.at[1])
    load_cent.start()
    load_emb.start()

    load_cent.wait()
    for p in range(PARTS):
        left = cent_v[:, 2 * W * p : 2 * W * p + W]
        right = cent_v[:, 2 * W * p + W : 2 * W * (p + 1)]
        first[p, x, HOME] = jnp.concatenate([left, right], axis=0).astype(BF16)
    load_emb.wait()
    own_rows = pl.ds(pl.multiple_of(cent * ROWS, ROWS), ROWS)
    rows[own_rows, :] = emb_v[...].astype(BF16)

    pl.semaphore_wait(barrier, (NZ - 1) + (NCENT - 1) + (NX - 1))

    def row_copy(owner, half, device, send):
        block = pl.ds(pl.multiple_of(owner * ROWS + half * HALF, HALF), HALF)
        return remote(
            rows.at[block, :],
            rows.at[block, :],
            rows_send_sem.at[send],
            rows_recv_sem.at[owner, half],
            device,
        )

    def owner_at(k):
        return lax.rem(y + k, NY) * NC + core

    up, down, far = owner_at(1), owner_at(3), owner_at(2)
    to_up, to_down, sibling = at_cent(up), at_cent(down), at_cent(y * NC + 1 - core)
    row_copy(cent, 0, to_up, 0).start()
    row_copy(cent, 1, to_down, 1).start()
    row_copy(cent, 0, sibling, 4).start()
    row_copy(cent, 1, sibling, 5).start()
    pending.append(lambda: [row_copy(cent, 0, sibling, k).wait_send() for k in range(2, 14)])

    def spread_z(buf, p, send, recv):
        for slot in reversed(range(HOME)):
            there = BACK[slot]
            remote(
                buf.at[p, x, HOME],
                buf.at[p, x, there],
                send.at[p],
                recv.at[p, there // PER],
                at_zx(z_peer(slot), x),
            ).start()

    def spread_x(buf, p, g, send, recv):
        group = pl.ds(g * PER, PER)
        take(buf.at[p, x, pl.ds(g * PER, PER - (g == GROUPS - 1))], recv[0].at[p, g])
        for k in (2, 1, 3):
            remote(
                buf.at[p, x, group],
                buf.at[p, x, group],
                send.at[p],
                recv[1].at[p],
                at_zx(z, lax.rem(x + k, NX)),
            ).start()

    def in_order(lag):
        pieces = [(p, g) for p in range(PARTS) for g in range(GROUPS)]
        return sorted(pieces, key=lambda piece: piece[0] + lag * (GROUPS - 1 - piece[1]))

    def each_part(body, start=0, stop=PARTS):
        def go(p, carry):
            body(p)
            return carry

        lax.fori_loop(start, stop, go, 0)

    each_part(lambda p: spread_z(first, p, gz_send, gz_recv))
    pending.append(lambda: each_part(lambda p: take(first.at[p, 0, pl.ds(0, NZ - 1)], gz_send.at[p])))

    row_copy(cent, 0, to_up, 0).wait_send()
    row_copy(cent, 1, to_up, 2).start()
    row_copy(cent, 1, to_down, 1).wait_send()
    row_copy(cent, 0, to_down, 3).start()

    steps = in_order(0.6)

    def spread_first(start, stop):
        for p, g in steps[start:stop]:
            spread_x(first, p, g, gx_send, (gz_recv, gx_recv))

    def chip_norms(k):
        chip = lax.rem(y + k, NY)
        for half in range(2):
            row_copy(chip * NC + 1 - core, half, sibling, 0).wait_recv()
        for j in range(CHIP_TILES):
            here = pl.ds(pl.multiple_of(chip * CHIP + j * LANES, LANES), LANES)
            part = jnp.zeros((LANES, LANES), F32)
            for i in range(D // LANES):
                block = rows[here, i * LANES : (i + 1) * LANES].astype(F32)
                part += block * block
            row_sq[:, here] = jnp.sum(part.T, axis=0, keepdims=True) * (1.0 / SCALE)

    spread_first(0, 2)
    row_copy(down, 0, sibling, 0).wait_recv()
    row_copy(down, 0, to_up, 6).start()
    row_copy(up, 1, sibling, 0).wait_recv()
    row_copy(up, 1, to_down, 7).start()
    row_copy(down, 0, sibling, 8).start()
    row_copy(up, 1, sibling, 9).start()
    spread_first(2, 8)
    row_copy(down, 1, sibling, 0).wait_recv()
    row_copy(down, 1, sibling, 10).start()
    row_copy(up, 0, sibling, 0).wait_recv()
    row_copy(up, 0, sibling, 11).start()
    spread_first(8, 12)
    norm_part[...] = jnp.zeros_like(norm_part)
    acc[...] = jnp.zeros_like(acc)
    chip_norms(0)
    spread_first(12, 16)
    pending.append(lambda: each_part(lambda p: take(first.at[p, pl.ds(0, NX - 1)], gx_send.at[p])))
    chip_norms(1)
    chip_norms(3)
    for half in range(2):
        row_copy(far, half, sibling, 0).wait_recv()
        row_copy(far, half, sibling, 12 + half).start()
    chip_norms(2)

    def products(buf, recv):
        def part(p):
            take(buf.at[p, pl.ds(0, NX - 1)], recv.at[p])
            lo = pl.ds(pl.multiple_of(2 * W * p, 2 * W), W)
            hi = pl.ds(pl.multiple_of(2 * W * p + W, W), W)
            both = pl.ds(pl.multiple_of(2 * W * p, 2 * W), 2 * W)
            for i in range(NX):
                block = buf[p, i].astype(F32)
                left = block[:, :OWN].reshape(NZ * OWN, W)
                right = block[:, OWN:].reshape(NZ * OWN, W)
                here = slice(i * NZ * OWN, (i + 1) * NZ * OWN)
                operand[here, lo] = left.astype(BF16)
                operand[here, hi] = right.astype(BF16)
                norm_part[here, :] += left * left + right * right
            acc[...] += lax.dot_general(
                operand[:, both],
                rows[:, both],
                (((1,), (1,)), ((), ())),
                preferred_element_type=F32,
            )

        each_part(part)
        norm[...] = jnp.broadcast_to(
            jnp.sum(norm_part[...] * (1.0 / SCALE), axis=1, keepdims=True), (SLICE, LANES)
        )

    products(first, gx_recv)

    def score_at(here):
        return (acc[:, here] * (2.0 / SCALE) - row_sq[:, here]) - norm[...]

    def tile(t):
        return slice(t * LANES, (t + 1) * LANES)

    for h in range(2):
        for j in range(TILES // 2):
            here = tile(h * (TILES // 2) + j)
            score = score_at(here)
            top = jnp.max(score, axis=0, keepdims=True)
            weight = jnp.exp(score - top)
            acc[:, here] = weight
            r = j % 3
            stat_send[h, j // 3, r : r + 1, :] = top
            stat_send[h, j // 3, 4 + r : 5 + r, :] = jnp.sum(weight, axis=0, keepdims=True)
        for k in range(1, NCENT):
            remote(
                stat_send.at[h],
                stat_recv.at[h, cent],
                st_send.at[h],
                st_recv.at[h],
                at_cent(lax.rem(cent + k, NCENT)),
            ).start()
        stat_recv[h, cent] = stat_send[h]
    pending.append(
        lambda: [take(stat_recv.at[h, pl.ds(0, NCENT - 1)], st_send.at[h]) for h in range(2)]
    )
    for h in range(2):
        take(stat_recv.at[h, pl.ds(0, NCENT - 1)], st_recv.at[h])
        tops = [stat_recv[h, s, :, 0:3, :] for s in range(NCENT)]
        top = tops[0]
        for s in range(1, NCENT):
            top = jnp.maximum(top, tops[s])
        total = jnp.zeros_like(top)
        for s in range(NCENT):
            total += stat_recv[h, s, :, 4:7, :] * jnp.exp(tops[s] - top)
        factor[h, :, 0:3, :] = jnp.exp(stat_send[h, :, 0:3, :] - top) / total
        for j in range(TILES // 2):
            here = tile(h * (TILES // 2) + j)
            r = j % 3
            resp[:, here] = (acc[:, here] * factor[h, j // 3, r : r + 1, :]).astype(BF16)

    def sums_x(p):
        both = pl.ds(pl.multiple_of(2 * W * p, 2 * W), 2 * W)
        value = jnp.dot(resp[...], rows[:, both], preferred_element_type=F32)
        for i in range(NX):
            block = value[i * NZ * OWN : (i + 1) * NZ * OWN]
            left = block[:, :W].reshape(NZ, OWN, W)
            right = block[:, W:].reshape(NZ, OWN, W)
            packed = jnp.concatenate([left, right], axis=1)
            sums_f[p, i] = packed
            sums_send[p, i] = packed.astype(BF16)
        for g in range(GROUPS):
            group = pl.ds(g * PER, PER)
            for k in (2, 1, 3):
                to = lax.rem(x + k, NX)
                remote(
                    sums_send.at[p, to, group],
                    sums_recv.at[p, x, group],
                    cx_send.at[p],
                    cx_recv.at[p, g],
                    at_zx(z, to),
                ).start()

    each_part(sums_x, 0, 1)

    mass_part = jnp.zeros((SLICE, LANES), F32)
    for t in range(TILES):
        mass_part += resp[:, t * LANES : (t + 1) * LANES].astype(F32)
    norm_part[...] = mass_part
    lane = lax.broadcasted_iota(jnp.int32, (NZ, OWN, LANES), 2)
    layer = lax.broadcasted_iota(jnp.int32, (NZ, OWN, LANES), 0)
    for i in range(NX):
        mass = jnp.sum(norm_part[i * NZ * OWN : (i + 1) * NZ * OWN, :], axis=1, keepdims=True)
        mass = jnp.broadcast_to(mass, (NZ * OWN, LANES)).reshape(NZ, OWN, LANES)
        count_send[i] = jnp.sum(jnp.where(lane == layer, mass, 0.0), axis=0)
    for k in (2, 1, 3):
        to = lax.rem(x + k, NX)
        remote(
            count_send.at[to], count_recv.at[x], nx_send.at[0], nx_recv.at[0], at_zx(z, to)
        ).start()
    pending.append(lambda: take(count_recv.at[pl.ds(0, NX - 1)], nx_send.at[0]))
    count_recv[x] = count_send[x]

    each_part(sums_x, 1, PARTS)
    pending.append(lambda: each_part(lambda p: take(sums_recv.at[p, pl.ds(0, NX - 1)], cx_send.at[p])))

    def sums_z(p):
        for g in range(GROUPS):
            group = slice(g * PER, (g + 1) * PER)
            take(sums_recv.at[p, pl.ds(0, NX - 1), pl.ds(g * PER, PER)], cx_recv.at[p, g])
            value = sums_f[p, x, group]
            for k in range(1, NX):
                value += sums_recv[p, lax.rem(x + k, NX), group].astype(F32)
            part_send[p, group] = value.astype(BF16)
            for slot in range(g * PER, (g + 1) * PER):
                if slot != HOME:
                    remote(
                        part_send.at[p, slot],
                        part_recv.at[p, BACK[slot]],
                        cz_send.at[p],
                        cz_recv.at[p],
                        at_zx(z_peer(slot), x),
                    ).start()
        part_recv[p, HOME] = part_send[p, HOME]

    each_part(sums_z, 0, 2)

    take(count_recv.at[pl.ds(0, NX - 1)], nx_recv.at[0])
    total_send[...] = (count_recv[0] + count_recv[1]) + (count_recv[2] + count_recv[3])
    for slot in range(HOME):
        remote(
            total_send,
            total_recv.at[BACK[slot]],
            nz_send.at[0],
            nz_recv.at[0],
            at_zx(z_peer(slot), x),
        ).start()
    pending.append(lambda: take(total_recv.at[pl.ds(0, NZ - 1)], nz_send.at[0]))
    total_recv[HOME] = total_send[...]

    each_part(sums_z, 2, PARTS)
    pending.append(lambda: each_part(lambda p: take(part_recv.at[p, pl.ds(0, NZ - 1)], cz_send.at[p])))

    norm_part[...] = jnp.zeros_like(norm_part)
    acc[...] = jnp.zeros_like(acc)

    take(total_recv.at[pl.ds(0, NZ - 1)], nz_recv.at[0])
    lane = lax.broadcasted_iota(jnp.int32, (OWN, LANES), 1)
    mass = jnp.zeros((OWN, LANES), F32)
    for slot in range(NZ):
        mass += jnp.where(lane == BACK[slot], total_recv[slot], 0.0)
    mass = jnp.sum(mass, axis=1, keepdims=True) + prior_mass

    def renew(p):
        take(part_recv.at[p, pl.ds(0, NZ - 1)], cz_recv.at[p])
        value = jnp.sum(part_recv[p].astype(F32), axis=0)
        lo = pl.ds(pl.multiple_of(2 * W * p, 2 * W), W)
        hi = pl.ds(pl.multiple_of(2 * W * p + W, W), W)
        left = (value[:OWN] + prior_mass * cent_v[:, lo]) / mass
        right = (value[OWN:] + prior_mass * cent_v[:, hi]) / mass
        upd_out[:, lo] = left
        upd_out[:, hi] = right
        second[p, x, HOME] = jnp.concatenate([left, right], axis=0).astype(BF16)
        spread_z(second, p, uz_send, uz_recv)

    each_part(renew)
    for p in range(PARTS):
        for g in reversed(range(GROUPS)):
            spread_x(second, p, g, ux_send, (uz_recv, ux_recv))
    pending.append(lambda: each_part(lambda p: take(second.at[p, 0, pl.ds(0, NZ - 1)], uz_send.at[p])))
    pending.append(lambda: each_part(lambda p: take(second.at[p, pl.ds(0, NX - 1)], ux_send.at[p])))
    products(second, ux_recv)

    for k in (2, 1, 3, 0):
        chip = lax.rem(y + k, NY)
        for j in range(CHIP_TILES):
            here = pl.ds(pl.multiple_of(chip * CHIP + j * LANES, LANES), LANES)
            score = score_at(here)
            top = jnp.max(score, axis=0, keepdims=True)
            shifted = score - top
            weight = jnp.exp(shifted)
            stat2_send[k, j, 0:1, :] = top
            stat2_send[k, j, 1:2, :] = jnp.sum(weight, axis=0, keepdims=True)
            stat2_send[k, j, 2:3, :] = jnp.sum(weight * shifted, axis=0, keepdims=True)
        targets = (chip * NC + core, chip * NC + 1 - core) if k else (chip * NC + 1 - core,)
        for to in targets:
            remote(
                stat2_send.at[k], stat2_recv.at[cent], st2_send.at[0], st2_recv.at[0], at_cent(to)
            ).start()
    pending.append(lambda: take(stat2_recv.at[pl.ds(0, NCENT - 1)], st2_send.at[0]))
    stat2_recv[cent] = stat2_send[0]
    finish()
    take(stat2_recv.at[pl.ds(0, NCENT - 1)], st2_recv.at[0])
    tops = [stat2_recv[s, :, 0:1, :] for s in range(NCENT)]
    top = tops[0]
    for s in range(1, NCENT):
        top = jnp.maximum(top, tops[s])
    total = jnp.zeros_like(top)
    spread = jnp.zeros_like(top)
    for s in range(NCENT):
        gap = tops[s] - top
        scale = jnp.exp(gap)
        mine = stat2_recv[s, :, 1:2, :]
        total += scale * mine
        spread += scale * (stat2_recv[s, :, 2:3, :] + gap * mine)
    ent_out[...] = jnp.log(total) - spread / total


def on_device(embeddings, centroids):
    vmem = pltpu.VMEM
    dma = pltpu.SemaphoreType.DMA
    gathered = (PARTS, NX, NZ, 2 * OWN, W)
    updated, entropy = pl.pallas_call(
        kernel,
        out_shape=(
            jax.ShapeDtypeStruct((OWN, D), F32),
            jax.ShapeDtypeStruct((CHIP_TILES, 1, LANES), F32),
        ),
        in_specs=[pl.BlockSpec(memory_space=pl.ANY)] * 2,
        out_specs=(pl.BlockSpec(memory_space=vmem), pl.BlockSpec(memory_space=vmem)),
        scratch_shapes=[
            vmem((ROWS, D), F32),
            vmem((OWN, D), F32),
            vmem((GROUP, D), BF16),
            vmem(gathered, BF16),
            vmem(gathered, BF16),
            vmem((SLICE, D), BF16),
            vmem((SLICE, LANES), F32),
            vmem((SLICE, LANES), F32),
            vmem((1, GROUP), F32),
            vmem((SLICE, GROUP), F32),
            vmem((SLICE, GROUP), BF16),
            vmem((2, 2, 8, LANES), F32),
            vmem((2, NCENT, 2, 8, LANES), F32),
            vmem((2, 2, 8, LANES), F32),
            vmem((NY, CHIP_TILES, 8, LANES), F32),
            vmem((NCENT, CHIP_TILES, 8, LANES), F32),
            vmem(gathered, F32),
            vmem(gathered, BF16),
            vmem(gathered, BF16),
            vmem((PARTS, NZ, 2 * OWN, W), BF16),
            vmem((PARTS, NZ, 2 * OWN, W), BF16),
            vmem((NX, OWN, LANES), F32),
            vmem((NX, OWN, LANES), F32),
            vmem((OWN, LANES), F32),
            vmem((NZ, OWN, LANES), F32),
            dma((2,)),
            dma((14,)),
            dma((NCENT, 2)),
            dma((PARTS,)),
            dma((PARTS, GROUPS)),
            dma((PARTS,)),
            dma((PARTS,)),
            dma((2,)),
            dma((2,)),
            dma((PARTS,)),
            dma((PARTS, GROUPS)),
            dma((PARTS,)),
            dma((PARTS,)),
            dma((1,)),
            dma((1,)),
            dma((1,)),
            dma((1,)),
            dma((PARTS,)),
            dma((PARTS, GROUPS)),
            dma((PARTS,)),
            dma((PARTS,)),
            dma((1,)),
            dma((1,)),
        ],
        compiler_params=pltpu.CompilerParams(
            collective_id=0, has_side_effects=True, vmem_limit_bytes=63 * 2**20
        ),
        name="em_update",
    )(embeddings, centroids)
    core = lax.axis_index("cent") % NC
    entropy = lax.dynamic_slice_in_dim(entropy.reshape(CHIP), core * ROWS, ROWS, 0)
    return updated, entropy


def solution(mesh):
    in_specs = (P(("dp", "cent"), None), P(("dp", "cent"), None))
    out_specs = (P(("dp", "cent"), None), P(("dp", "cent")))
    return jax.shard_map(
        on_device, mesh=mesh, in_specs=in_specs, out_specs=out_specs, check_vma=False
    )
```

```python
import jax
import jax.numpy as jnp
from jax import lax
from jax.experimental import pallas as pl
from jax.experimental.pallas import tpu as pltpu
from jax.sharding import PartitionSpec as P

MESH = pl.DeviceIdType.MESH
F32 = jnp.float32
BF16 = jnp.bfloat16

softness_level = 32.0
prior_mass = 4.0

D = 1024
NZ, NX, NY, NC = 16, 4, 4, 2
NCENT = NY * NC
ROWS = 192
GROUP = ROWS * NCENT
CHIP = ROWS * NC
OWN = 8
SLICE = OWN * NZ * NX
PARTS = 4
W = D // (2 * PARTS)
LANES = 128
TILES = GROUP // LANES
CHIP_TILES = CHIP // LANES
SCALE = 2.0 * softness_level
OFFSETS = (8, 7, 9, 6, 10, 5, 11, 4, 12, 3, 13, 2, 14, 1, 15, 0)
SLOT = {offset: slot for slot, offset in enumerate(OFFSETS)}
BACK = tuple(SLOT[(NZ - offset) % NZ] for offset in OFFSETS)
GROUPS = 4
PER = NZ // GROUPS
HOME = NZ - 1
HALF = ROWS // 2


def place():
    dp = lax.axis_index("dp")
    cent = lax.axis_index("cent")
    z = dp // NX
    x = dp % NX
    y = cent // NC
    core = cent % NC
    return z, x, y, core, cent


def kernel(
    emb_hbm,
    cent_hbm,
    upd_out,
    ent_out,
    emb_v,
    cent_v,
    rows,
    first,
    second,
    operand,
    norm_part,
    norm,
    row_sq,
    acc,
    resp,
    stat_send,
    stat_recv,
    factor,
    stat2_send,
    stat2_recv,
    sums_f,
    sums_send,
    sums_recv,
    part_send,
    part_recv,
    count_send,
    count_recv,
    total_send,
    total_recv,
    load_sem,
    rows_send_sem,
    rows_recv_sem,
    gz_send,
    gz_recv,
    gx_send,
    gx_recv,
    st_send,
    st_recv,
    cx_send,
    cx_recv,
    cz_send,
    cz_recv,
    nx_send,
    nx_recv,
    nz_send,
    nz_recv,
    uz_send,
    uz_recv,
    ux_send,
    ux_recv,
    st2_send,
    st2_recv,
):
    z, x, y, core, cent = place()

    def at_zx(z_to, x_to):
        return {"dp": z_to * NX + x_to, "cent": cent}

    def at_cent(cent_to):
        return {"dp": z * NX + x, "cent": cent_to}

    def remote(src, dst, send, recv, device):
        return pltpu.make_async_remote_copy(
            src_ref=src, dst_ref=dst, send_sem=send, recv_sem=recv, device_id=device, device_id_type=MESH
        )

    def take(ref, sem):
        pltpu.make_async_copy(ref, ref, sem).wait()

    pending = []

    def finish():
        for wait in pending:
            wait()

    def z_peer(slot):
        return lax.rem(z + OFFSETS[slot], NZ)

    barrier = pltpu.get_barrier_semaphore()
    for slot in range(HOME):
        pl.semaphore_signal(
            barrier, inc=1, device_id=at_zx(z_peer(slot), x), device_id_type=MESH
        )
    for k in range(1, NCENT):
        pl.semaphore_signal(
            barrier, inc=1, device_id=at_cent((cent + k) % NCENT), device_id_type=MESH
        )
    for k in range(1, NX):
        pl.semaphore_signal(barrier, inc=1, device_id=at_zx(z, (x + k) % NX), device_id_type=MESH)

    load_cent = pltpu.make_async_copy(cent_hbm, cent_v, load_sem.at[0])
    load_emb = pltpu.make_async_copy(emb_hbm, emb_v, load_sem.at[1])
    load_cent.start()
    load_emb.start()

    load_cent.wait()
    for p in range(PARTS):
        left = cent_v[:, 2 * W * p : 2 * W * p + W]
        right = cent_v[:, 2 * W * p + W : 2 * W * (p + 1)]
        first[p, x, HOME] = jnp.concatenate([left, right], axis=0).astype(BF16)
    load_emb.wait()
    own_rows = pl.ds(pl.multiple_of(cent * ROWS, ROWS), ROWS)
    rows[own_rows, :] = emb_v[...].astype(BF16)

    pl.semaphore_wait(barrier, (NZ - 1) + (NCENT - 1) + (NX - 1))

    def row_copy(owner, half, device, send):
        block = pl.ds(pl.multiple_of(owner * ROWS + half * HALF, HALF), HALF)
        return remote(
            rows.at[block, :],
            rows.at[block, :],
            rows_send_sem.at[send],
            rows_recv_sem.at[owner, half],
            device,
        )

    def owner_at(k):
        return lax.rem(y + k, NY) * NC + core

    up, down, far = owner_at(1), owner_at(3), owner_at(2)
    to_up, to_down, sibling = at_cent(up), at_cent(down), at_cent(y * NC + 1 - core)
    row_copy(cent, 0, to_up, 0).start()
    row_copy(cent, 1, to_down, 1).start()
    row_copy(cent, 0, sibling, 4).start()
    row_copy(cent, 1, sibling, 5).start()
    pending.append(lambda: [row_copy(cent, 0, sibling, k).wait_send() for k in range(2, 14)])

    def spread_z(buf, p, send, recv):
        for slot in reversed(range(HOME)):
            there = BACK[slot]
            remote(
                buf.at[p, x, HOME],
                buf.at[p, x, there],
                send.at[p],
                recv.at[p, there // PER],
                at_zx(z_peer(slot), x),
            ).start()

    def spread_x(buf, p, g, send, recv):
        group = pl.ds(g * PER, PER)
        take(buf.at[p, x, pl.ds(g * PER, PER - (g == GROUPS - 1))], recv[0].at[p, g])
        for k in (2, 1, 3):
            remote(
                buf.at[p, x, group],
                buf.at[p, x, group],
                send.at[p],
                recv[1].at[p],
                at_zx(z, lax.rem(x + k, NX)),
            ).start()

    def in_order(lag):
        pieces = [(p, g) for p in range(PARTS) for g in range(GROUPS)]
        return sorted(pieces, key=lambda piece: piece[0] + lag * (GROUPS - 1 - piece[1]))

    def each_part(body, start=0, stop=PARTS):
        def go(p, carry):
            body(p)
            return carry

        lax.fori_loop(start, stop, go, 0)

    each_part(lambda p: spread_z(first, p, gz_send, gz_recv))
    pending.append(lambda: each_part(lambda p: take(first.at[p, 0, pl.ds(0, NZ - 1)], gz_send.at[p])))

    row_copy(cent, 0, to_up, 0).wait_send()
    row_copy(cent, 1, to_up, 2).start()
    row_copy(cent, 1, to_down, 1).wait_send()
    row_copy(cent, 0, to_down, 3).start()

    steps = in_order(0.6)

    def spread_first(start, stop):
        for p, g in steps[start:stop]:
            spread_x(first, p, g, gx_send, (gz_recv, gx_recv))

    def chip_norms(k):
        chip = lax.rem(y + k, NY)
        for half in range(2):
            row_copy(chip * NC + 1 - core, half, sibling, 0).wait_recv()
        for j in range(CHIP_TILES):
            here = pl.ds(pl.multiple_of(chip * CHIP + j * LANES, LANES), LANES)
            part = jnp.zeros((LANES, LANES), F32)
            for i in range(D // LANES):
                block = rows[here, i * LANES : (i + 1) * LANES].astype(F32)
                part += block * block
            row_sq[:, here] = jnp.sum(part.T, axis=0, keepdims=True) * (1.0 / SCALE)

    spread_first(0, 2)
    row_copy(down, 0, sibling, 0).wait_recv()
    row_copy(down, 0, to_up, 6).start()
    row_copy(up, 1, sibling, 0).wait_recv()
    row_copy(up, 1, to_down, 7).start()
    row_copy(down, 0, sibling, 8).start()
    row_copy(up, 1, sibling, 9).start()
    spread_first(2, 8)
    row_copy(down, 1, sibling, 0).wait_recv()
    row_copy(down, 1, sibling, 10).start()
    row_copy(up, 0, sibling, 0).wait_recv()
    row_copy(up, 0, sibling, 11).start()
    spread_first(8, 12)
    norm_part[...] = jnp.zeros_like(norm_part)
    acc[...] = jnp.zeros_like(acc)
    chip_norms(0)
    spread_first(12, 16)
    pending.append(lambda: each_part(lambda p: take(first.at[p, pl.ds(0, NX - 1)], gx_send.at[p])))
    chip_norms(1)
    chip_norms(3)
    for half in range(2):
        row_copy(far, half, sibling, 0).wait_recv()
        row_copy(far, half, sibling, 12 + half).start()
    chip_norms(2)

    def products(buf, recv):
        def part(p):
            take(buf.at[p, pl.ds(0, NX - 1)], recv.at[p])
            lo = pl.ds(pl.multiple_of(2 * W * p, 2 * W), W)
            hi = pl.ds(pl.multiple_of(2 * W * p + W, W), W)
            both = pl.ds(pl.multiple_of(2 * W * p, 2 * W), 2 * W)
            for i in range(NX):
                block = buf[p, i].astype(F32)
                left = block[:, :OWN].reshape(NZ * OWN, W)
                right = block[:, OWN:].reshape(NZ * OWN, W)
                here = slice(i * NZ * OWN, (i + 1) * NZ * OWN)
                operand[here, lo] = left.astype(BF16)
                operand[here, hi] = right.astype(BF16)
                norm_part[here, :] += left * left + right * right
            acc[...] += lax.dot_general(
                operand[:, both],
                rows[:, both],
                (((1,), (1,)), ((), ())),
                preferred_element_type=F32,
            )

        each_part(part)
        norm[...] = jnp.broadcast_to(
            jnp.sum(norm_part[...] * (1.0 / SCALE), axis=1, keepdims=True), (SLICE, LANES)
        )

    products(first, gx_recv)

    def score_at(here):
        return (acc[:, here] * (2.0 / SCALE) - row_sq[:, here]) - norm[...]

    def tile(t):
        return slice(t * LANES, (t + 1) * LANES)

    for h in range(2):
        for j in range(TILES // 2):
            here = tile(h * (TILES // 2) + j)
            score = score_at(here)
            top = jnp.max(score, axis=0, keepdims=True)
            weight = jnp.exp(score - top)
            acc[:, here] = weight
            r = j % 3
            stat_send[h, j // 3, r : r + 1, :] = top
            stat_send[h, j // 3, 4 + r : 5 + r, :] = jnp.sum(weight, axis=0, keepdims=True)
        for k in range(1, NCENT):
            remote(
                stat_send.at[h],
                stat_recv.at[h, cent],
                st_send.at[h],
                st_recv.at[h],
                at_cent(lax.rem(cent + k, NCENT)),
            ).start()
        stat_recv[h, cent] = stat_send[h]
    pending.append(
        lambda: [take(stat_recv.at[h, pl.ds(0, NCENT - 1)], st_send.at[h]) for h in range(2)]
    )
    for h in range(2):
        take(stat_recv.at[h, pl.ds(0, NCENT - 1)], st_recv.at[h])
        tops = [stat_recv[h, s, :, 0:3, :] for s in range(NCENT)]
        top = tops[0]
        for s in range(1, NCENT):
            top = jnp.maximum(top, tops[s])
        total = jnp.zeros_like(top)
        for s in range(NCENT):
            total += stat_recv[h, s, :, 4:7, :] * jnp.exp(tops[s] - top)
        factor[h, :, 0:3, :] = jnp.exp(stat_send[h, :, 0:3, :] - top) / total
        for j in range(TILES // 2):
            here = tile(h * (TILES // 2) + j)
            r = j % 3
            resp[:, here] = (acc[:, here] * factor[h, j // 3, r : r + 1, :]).astype(BF16)

    def sums_x(p):
        both = pl.ds(pl.multiple_of(2 * W * p, 2 * W), 2 * W)
        value = jnp.dot(resp[...], rows[:, both], preferred_element_type=F32)
        for i in range(NX):
            block = value[i * NZ * OWN : (i + 1) * NZ * OWN]
            left = block[:, :W].reshape(NZ, OWN, W)
            right = block[:, W:].reshape(NZ, OWN, W)
            packed = jnp.concatenate([left, right], axis=1)
            sums_f[p, i] = packed
            sums_send[p, i] = packed.astype(BF16)
        for g in range(GROUPS):
            group = pl.ds(g * PER, PER)
            for k in (2, 1, 3):
                to = lax.rem(x + k, NX)
                remote(
                    sums_send.at[p, to, group],
                    sums_recv.at[p, x, group],
                    cx_send.at[p],
                    cx_recv.at[p, g],
                    at_zx(z, to),
                ).start()

    each_part(sums_x, 0, 1)

    mass_part = jnp.zeros((SLICE, LANES), F32)
    for t in range(TILES):
        mass_part += resp[:, t * LANES : (t + 1) * LANES].astype(F32)
    norm_part[...] = mass_part
    block = (NZ * OWN, LANES)
    diagonal = lax.broadcasted_iota(jnp.int32, block, 0) == lax.broadcasted_iota(jnp.int32, block, 1)
    for i in range(NX):
        mass = jnp.sum(norm_part[i * NZ * OWN : (i + 1) * NZ * OWN, :], axis=1, keepdims=True)
        count_send[i] = jnp.sum(jnp.where(diagonal, mass, 0.0), axis=0, keepdims=True)
    for k in (2, 1, 3):
        to = lax.rem(x + k, NX)
        remote(
            count_send.at[to], count_recv.at[x], nx_send.at[0], nx_recv.at[0], at_zx(z, to)
        ).start()
    pending.append(lambda: take(count_recv.at[pl.ds(0, NX - 1)], nx_send.at[0]))
    count_recv[x] = count_send[x]

    each_part(sums_x, 1, PARTS)
    pending.append(lambda: each_part(lambda p: take(sums_recv.at[p, pl.ds(0, NX - 1)], cx_send.at[p])))

    def sums_z(p):
        for g in range(GROUPS):
            group = slice(g * PER, (g + 1) * PER)
            take(sums_recv.at[p, pl.ds(0, NX - 1), pl.ds(g * PER, PER)], cx_recv.at[p, g])
            value = sums_f[p, x, group]
            for k in range(1, NX):
                value += sums_recv[p, lax.rem(x + k, NX), group].astype(F32)
            part_send[p, group] = value.astype(BF16)
            for slot in range(g * PER, (g + 1) * PER):
                if slot != HOME:
                    remote(
                        part_send.at[p, slot],
                        part_recv.at[p, BACK[slot]],
                        cz_send.at[p],
                        cz_recv.at[p],
                        at_zx(z_peer(slot), x),
                    ).start()
        part_recv[p, HOME] = part_send[p, HOME]

    each_part(sums_z, 0, 2)

    take(count_recv.at[pl.ds(0, NX - 1)], nx_recv.at[0])
    total_send[...] = (count_recv[0] + count_recv[1]) + (count_recv[2] + count_recv[3])
    for slot in range(HOME):
        remote(
            total_send,
            total_recv.at[BACK[slot]],
            nz_send.at[0],
            nz_recv.at[0],
            at_zx(z_peer(slot), x),
        ).start()
    pending.append(lambda: take(total_recv.at[pl.ds(0, NZ - 1)], nz_send.at[0]))
    total_recv[HOME] = total_send[...]

    each_part(sums_z, 2, PARTS)
    pending.append(lambda: each_part(lambda p: take(part_recv.at[p, pl.ds(0, NZ - 1)], cz_send.at[p])))

    norm_part[...] = jnp.zeros_like(norm_part)
    acc[...] = jnp.zeros_like(acc)

    take(total_recv.at[pl.ds(0, NZ - 1)], nz_recv.at[0])
    row = lax.broadcasted_iota(jnp.int32, (OWN, LANES), 0)
    lane = lax.broadcasted_iota(jnp.int32, (OWN, LANES), 1)
    mass = jnp.zeros((OWN, LANES), F32)
    for slot in range(NZ):
        mass += jnp.where(lane == BACK[slot] * OWN + row, total_recv[slot], 0.0)
    mass = jnp.sum(mass, axis=1, keepdims=True) + prior_mass

    def renew(p):
        take(part_recv.at[p, pl.ds(0, NZ - 1)], cz_recv.at[p])
        value = jnp.sum(part_recv[p].astype(F32), axis=0)
        lo = pl.ds(pl.multiple_of(2 * W * p, 2 * W), W)
        hi = pl.ds(pl.multiple_of(2 * W * p + W, W), W)
        left = (value[:OWN] + prior_mass * cent_v[:, lo]) / mass
        right = (value[OWN:] + prior_mass * cent_v[:, hi]) / mass
        upd_out[:, lo] = left
        upd_out[:, hi] = right
        second[p, x, HOME] = jnp.concatenate([left, right], axis=0).astype(BF16)
        spread_z(second, p, uz_send, uz_recv)

    each_part(renew)
    for p in range(PARTS):
        for g in reversed(range(GROUPS)):
            spread_x(second, p, g, ux_send, (uz_recv, ux_recv))
    pending.append(lambda: each_part(lambda p: take(second.at[p, 0, pl.ds(0, NZ - 1)], uz_send.at[p])))
    pending.append(lambda: each_part(lambda p: take(second.at[p, pl.ds(0, NX - 1)], ux_send.at[p])))
    products(second, ux_recv)

    for k in (2, 1, 3, 0):
        chip = lax.rem(y + k, NY)
        for j in range(CHIP_TILES):
            here = pl.ds(pl.multiple_of(chip * CHIP + j * LANES, LANES), LANES)
            score = score_at(here)
            top = jnp.max(score, axis=0, keepdims=True)
            shifted = score - top
            weight = jnp.exp(shifted)
            stat2_send[k, j, 0:1, :] = top
            stat2_send[k, j, 1:2, :] = jnp.sum(weight, axis=0, keepdims=True)
            stat2_send[k, j, 2:3, :] = jnp.sum(weight * shifted, axis=0, keepdims=True)
        targets = (chip * NC + core, chip * NC + 1 - core) if k else (chip * NC + 1 - core,)
        for to in targets:
            remote(
                stat2_send.at[k], stat2_recv.at[cent], st2_send.at[0], st2_recv.at[0], at_cent(to)
            ).start()
    pending.append(lambda: take(stat2_recv.at[pl.ds(0, NCENT - 1)], st2_send.at[0]))
    stat2_recv[cent] = stat2_send[0]
    finish()
    take(stat2_recv.at[pl.ds(0, NCENT - 1)], st2_recv.at[0])
    tops = [stat2_recv[s, :, 0:1, :] for s in range(NCENT)]
    top = tops[0]
    for s in range(1, NCENT):
        top = jnp.maximum(top, tops[s])
    total = jnp.zeros_like(top)
    spread = jnp.zeros_like(top)
    for s in range(NCENT):
        gap = tops[s] - top
        scale = jnp.exp(gap)
        mine = stat2_recv[s, :, 1:2, :]
        total += scale * mine
        spread += scale * (stat2_recv[s, :, 2:3, :] + gap * mine)
    ent_out[...] = jnp.log(total) - spread / total


def on_device(embeddings, centroids):
    vmem = pltpu.VMEM
    dma = pltpu.SemaphoreType.DMA
    gathered = (PARTS, NX, NZ, 2 * OWN, W)
    updated, entropy = pl.pallas_call(
        kernel,
        out_shape=(
            jax.ShapeDtypeStruct((OWN, D), F32),
            jax.ShapeDtypeStruct((CHIP_TILES, 1, LANES), F32),
        ),
        in_specs=[pl.BlockSpec(memory_space=pl.ANY)] * 2,
        out_specs=(pl.BlockSpec(memory_space=vmem), pl.BlockSpec(memory_space=vmem)),
        scratch_shapes=[
            vmem((ROWS, D), F32),
            vmem((OWN, D), F32),
            vmem((GROUP, D), BF16),
            vmem(gathered, BF16),
            vmem(gathered, BF16),
            vmem((SLICE, D), BF16),
            vmem((SLICE, LANES), F32),
            vmem((SLICE, LANES), F32),
            vmem((1, GROUP), F32),
            vmem((SLICE, GROUP), F32),
            vmem((SLICE, GROUP), BF16),
            vmem((2, 2, 8, LANES), F32),
            vmem((2, NCENT, 2, 8, LANES), F32),
            vmem((2, 2, 8, LANES), F32),
            vmem((NY, CHIP_TILES, 8, LANES), F32),
            vmem((NCENT, CHIP_TILES, 8, LANES), F32),
            vmem(gathered, F32),
            vmem(gathered, BF16),
            vmem(gathered, BF16),
            vmem((PARTS, NZ, 2 * OWN, W), BF16),
            vmem((PARTS, NZ, 2 * OWN, W), BF16),
            vmem((NX, 1, LANES), F32),
            vmem((NX, 1, LANES), F32),
            vmem((1, LANES), F32),
            vmem((NZ, 1, LANES), F32),
            dma((2,)),
            dma((14,)),
            dma((NCENT, 2)),
            dma((PARTS,)),
            dma((PARTS, GROUPS)),
            dma((PARTS,)),
            dma((PARTS,)),
            dma((2,)),
            dma((2,)),
            dma((PARTS,)),
            dma((PARTS, GROUPS)),
            dma((PARTS,)),
            dma((PARTS,)),
            dma((1,)),
            dma((1,)),
            dma((1,)),
            dma((1,)),
            dma((PARTS,)),
            dma((PARTS, GROUPS)),
            dma((PARTS,)),
            dma((PARTS,)),
            dma((1,)),
            dma((1,)),
        ],
        compiler_params=pltpu.CompilerParams(
            collective_id=0, has_side_effects=True, vmem_limit_bytes=63 * 2**20
        ),
        name="em_update",
    )(embeddings, centroids)
    core = lax.axis_index("cent") % NC
    entropy = lax.dynamic_slice_in_dim(entropy.reshape(CHIP), core * ROWS, ROWS, 0)
    return updated, entropy


def solution(mesh):
    in_specs = (P(("dp", "cent"), None), P(("dp", "cent"), None))
    out_specs = (P(("dp", "cent"), None), P(("dp", "cent")))
    return jax.shard_map(
        on_device, mesh=mesh, in_specs=in_specs, out_specs=out_specs, check_vma=False
    )
```

```python
import jax
import jax.numpy as jnp
from jax import lax
from jax.experimental import pallas as pl
from jax.experimental.pallas import tpu as pltpu
from jax.sharding import PartitionSpec as P

MESH = pl.DeviceIdType.MESH
F32 = jnp.float32
BF16 = jnp.bfloat16

softness_level = 32.0
prior_mass = 4.0

D = 1024
NZ, NX, NY, NC = 16, 4, 4, 2
NCENT = NY * NC
ROWS = 192
GROUP = ROWS * NCENT
CHIP = ROWS * NC
OWN = 8
SLICE = OWN * NZ * NX
PARTS = 4
W = D // (2 * PARTS)
LANES = 128
TILES = GROUP // LANES
CHIP_TILES = CHIP // LANES
SCALE = 2.0 * softness_level
OFFSETS = (8, 7, 9, 6, 10, 5, 11, 4, 12, 3, 13, 2, 14, 1, 15, 0)
SLOT = {offset: slot for slot, offset in enumerate(OFFSETS)}
BACK = tuple(SLOT[(NZ - offset) % NZ] for offset in OFFSETS)
GROUPS = 4
PER = NZ // GROUPS
SUM_GROUPS = 8
SUM_PER = NZ // SUM_GROUPS
HOME = NZ - 1
HALF = ROWS // 2


def place():
    dp = lax.axis_index("dp")
    cent = lax.axis_index("cent")
    z = dp // NX
    x = dp % NX
    y = cent // NC
    core = cent % NC
    return z, x, y, core, cent


def kernel(
    emb_hbm,
    cent_hbm,
    upd_out,
    ent_out,
    emb_v,
    cent_v,
    rows,
    first,
    second,
    operand,
    norm_part,
    norm,
    row_sq,
    acc,
    resp,
    stat_send,
    stat_recv,
    factor,
    stat2_send,
    stat2_recv,
    sums_f,
    sums_send,
    sums_recv,
    part_send,
    part_recv,
    count_send,
    count_recv,
    total_send,
    total_recv,
    load_sem,
    rows_send_sem,
    rows_recv_sem,
    gz_send,
    gz_recv,
    gx_send,
    gx_recv,
    st_send,
    st_recv,
    cx_send,
    cx_recv,
    cz_send,
    cz_recv,
    nx_send,
    nx_recv,
    nz_send,
    nz_recv,
    uz_send,
    uz_recv,
    ux_send,
    ux_recv,
    st2_send,
    st2_recv,
):
    z, x, y, core, cent = place()

    def at_zx(z_to, x_to):
        return {"dp": z_to * NX + x_to, "cent": cent}

    def at_cent(cent_to):
        return {"dp": z * NX + x, "cent": cent_to}

    def remote(src, dst, send, recv, device):
        return pltpu.make_async_remote_copy(
            src_ref=src, dst_ref=dst, send_sem=send, recv_sem=recv, device_id=device, device_id_type=MESH
        )

    def take(ref, sem):
        pltpu.make_async_copy(ref, ref, sem).wait()

    pending = []

    def finish():
        for wait in pending:
            wait()

    def z_peer(slot):
        return lax.rem(z + OFFSETS[slot], NZ)

    barrier = pltpu.get_barrier_semaphore()
    for slot in range(HOME):
        pl.semaphore_signal(
            barrier, inc=1, device_id=at_zx(z_peer(slot), x), device_id_type=MESH
        )
    for k in range(1, NCENT):
        pl.semaphore_signal(
            barrier, inc=1, device_id=at_cent((cent + k) % NCENT), device_id_type=MESH
        )
    for k in range(1, NX):
        pl.semaphore_signal(barrier, inc=1, device_id=at_zx(z, (x + k) % NX), device_id_type=MESH)

    load_cent = pltpu.make_async_copy(cent_hbm, cent_v, load_sem.at[0])
    load_emb = pltpu.make_async_copy(emb_hbm, emb_v, load_sem.at[1])
    load_cent.start()
    load_emb.start()

    load_cent.wait()
    for p in range(PARTS):
        left = cent_v[:, 2 * W * p : 2 * W * p + W]
        right = cent_v[:, 2 * W * p + W : 2 * W * (p + 1)]
        first[p, x, HOME] = jnp.concatenate([left, right], axis=0).astype(BF16)
    load_emb.wait()
    own_rows = pl.ds(pl.multiple_of(cent * ROWS, ROWS), ROWS)
    rows[own_rows, :] = emb_v[...].astype(BF16)

    pl.semaphore_wait(barrier, (NZ - 1) + (NCENT - 1) + (NX - 1))

    def row_copy(owner, half, device, send):
        block = pl.ds(pl.multiple_of(owner * ROWS + half * HALF, HALF), HALF)
        return remote(
            rows.at[block, :],
            rows.at[block, :],
            rows_send_sem.at[send],
            rows_recv_sem.at[owner, half],
            device,
        )

    def owner_at(k):
        return lax.rem(y + k, NY) * NC + core

    up, down, far = owner_at(1), owner_at(3), owner_at(2)
    to_up, to_down, sibling = at_cent(up), at_cent(down), at_cent(y * NC + 1 - core)
    row_copy(cent, 0, to_up, 0).start()
    row_copy(cent, 1, to_down, 1).start()
    row_copy(cent, 0, sibling, 4).start()
    row_copy(cent, 1, sibling, 5).start()
    pending.append(lambda: [row_copy(cent, 0, sibling, k).wait_send() for k in range(2, 14)])

    def spread_z(buf, p, send, recv):
        for slot in reversed(range(HOME)):
            there = BACK[slot]
            remote(
                buf.at[p, x, HOME],
                buf.at[p, x, there],
                send.at[p],
                recv.at[p, there // PER],
                at_zx(z_peer(slot), x),
            ).start()

    def spread_x(buf, p, g, send, recv):
        group = pl.ds(g * PER, PER)
        take(buf.at[p, x, pl.ds(g * PER, PER - (g == GROUPS - 1))], recv[0].at[p, g])
        for k in (2, 1, 3):
            remote(
                buf.at[p, x, group],
                buf.at[p, x, group],
                send.at[p],
                recv[1].at[p],
                at_zx(z, lax.rem(x + k, NX)),
            ).start()

    def in_order(lag):
        pieces = [(p, g) for p in range(PARTS) for g in range(GROUPS)]
        return sorted(pieces, key=lambda piece: piece[0] + lag * (GROUPS - 1 - piece[1]))

    def each_part(body, start=0, stop=PARTS):
        def go(p, carry):
            body(p)
            return carry

        lax.fori_loop(start, stop, go, 0)

    each_part(lambda p: spread_z(first, p, gz_send, gz_recv))
    pending.append(lambda: each_part(lambda p: take(first.at[p, 0, pl.ds(0, NZ - 1)], gz_send.at[p])))

    row_copy(cent, 0, to_up, 0).wait_send()
    row_copy(cent, 1, to_up, 2).start()
    row_copy(cent, 1, to_down, 1).wait_send()
    row_copy(cent, 0, to_down, 3).start()

    steps = in_order(0.6)

    def spread_first(start, stop):
        for p, g in steps[start:stop]:
            spread_x(first, p, g, gx_send, (gz_recv, gx_recv))

    def chip_norms(k):
        chip = lax.rem(y + k, NY)
        for half in range(2):
            row_copy(chip * NC + 1 - core, half, sibling, 0).wait_recv()
        for j in range(CHIP_TILES):
            here = pl.ds(pl.multiple_of(chip * CHIP + j * LANES, LANES), LANES)
            part = jnp.zeros((LANES, LANES), F32)
            for i in range(D // LANES):
                block = rows[here, i * LANES : (i + 1) * LANES].astype(F32)
                part += block * block
            row_sq[:, here] = jnp.sum(part.T, axis=0, keepdims=True) * (1.0 / SCALE)

    spread_first(0, 2)
    row_copy(down, 0, sibling, 0).wait_recv()
    row_copy(down, 0, to_up, 6).start()
    row_copy(up, 1, sibling, 0).wait_recv()
    row_copy(up, 1, to_down, 7).start()
    row_copy(down, 0, sibling, 8).start()
    row_copy(up, 1, sibling, 9).start()
    spread_first(2, 8)
    row_copy(down, 1, sibling, 0).wait_recv()
    row_copy(down, 1, sibling, 10).start()
    row_copy(up, 0, sibling, 0).wait_recv()
    row_copy(up, 0, sibling, 11).start()
    spread_first(8, 12)
    norm_part[...] = jnp.zeros_like(norm_part)
    acc[...] = jnp.zeros_like(acc)
    chip_norms(0)
    spread_first(12, 16)
    pending.append(lambda: each_part(lambda p: take(first.at[p, pl.ds(0, NX - 1)], gx_send.at[p])))
    chip_norms(1)
    chip_norms(3)
    for half in range(2):
        row_copy(far, half, sibling, 0).wait_recv()
        row_copy(far, half, sibling, 12 + half).start()
    chip_norms(2)

    def products(buf, recv):
        def part(p):
            take(buf.at[p, pl.ds(0, NX - 1)], recv.at[p])
            lo = pl.ds(pl.multiple_of(2 * W * p, 2 * W), W)
            hi = pl.ds(pl.multiple_of(2 * W * p + W, W), W)
            both = pl.ds(pl.multiple_of(2 * W * p, 2 * W), 2 * W)
            for i in range(NX):
                block = buf[p, i].astype(F32)
                left = block[:, :OWN].reshape(NZ * OWN, W)
                right = block[:, OWN:].reshape(NZ * OWN, W)
                here = slice(i * NZ * OWN, (i + 1) * NZ * OWN)
                operand[here, lo] = left.astype(BF16)
                operand[here, hi] = right.astype(BF16)
                norm_part[here, :] += left * left + right * right
            acc[...] += lax.dot_general(
                operand[:, both],
                rows[:, both],
                (((1,), (1,)), ((), ())),
                preferred_element_type=F32,
            )

        each_part(part)
        norm[...] = jnp.broadcast_to(
            jnp.sum(norm_part[...] * (1.0 / SCALE), axis=1, keepdims=True), (SLICE, LANES)
        )

    products(first, gx_recv)

    def score_at(here):
        return (acc[:, here] * (2.0 / SCALE) - row_sq[:, here]) - norm[...]

    def tile(t):
        return slice(t * LANES, (t + 1) * LANES)

    for h in range(2):
        for j in range(TILES // 2):
            here = tile(h * (TILES // 2) + j)
            score = score_at(here)
            top = jnp.max(score, axis=0, keepdims=True)
            weight = jnp.exp(score - top)
            acc[:, here] = weight
            r = j % 3
            stat_send[h, j // 3, r : r + 1, :] = top
            stat_send[h, j // 3, 4 + r : 5 + r, :] = jnp.sum(weight, axis=0, keepdims=True)
        for k in range(1, NCENT):
            remote(
                stat_send.at[h],
                stat_recv.at[h, cent],
                st_send.at[h],
                st_recv.at[h],
                at_cent(lax.rem(cent + k, NCENT)),
            ).start()
        stat_recv[h, cent] = stat_send[h]
    pending.append(
        lambda: [take(stat_recv.at[h, pl.ds(0, NCENT - 1)], st_send.at[h]) for h in range(2)]
    )
    for h in range(2):
        take(stat_recv.at[h, pl.ds(0, NCENT - 1)], st_recv.at[h])
        tops = [stat_recv[h, s, :, 0:3, :] for s in range(NCENT)]
        top = tops[0]
        for s in range(1, NCENT):
            top = jnp.maximum(top, tops[s])
        total = jnp.zeros_like(top)
        for s in range(NCENT):
            total += stat_recv[h, s, :, 4:7, :] * jnp.exp(tops[s] - top)
        factor[h, :, 0:3, :] = jnp.exp(stat_send[h, :, 0:3, :] - top) / total
        for j in range(TILES // 2):
            here = tile(h * (TILES // 2) + j)
            r = j % 3
            resp[:, here] = (acc[:, here] * factor[h, j // 3, r : r + 1, :]).astype(BF16)

    def sums_x(p):
        both = pl.ds(pl.multiple_of(2 * W * p, 2 * W), 2 * W)
        value = jnp.dot(resp[...], rows[:, both], preferred_element_type=F32)
        for i in range(NX):
            block = value[i * NZ * OWN : (i + 1) * NZ * OWN]
            left = block[:, :W].reshape(NZ, OWN, W)
            right = block[:, W:].reshape(NZ, OWN, W)
            packed = jnp.concatenate([left, right], axis=1)
            sums_f[p, i] = packed
            sums_send[p, i] = packed.astype(BF16)
        for g in range(SUM_GROUPS):
            group = pl.ds(g * SUM_PER, SUM_PER)
            for k in (2, 1, 3):
                to = lax.rem(x + k, NX)
                remote(
                    sums_send.at[p, to, group],
                    sums_recv.at[p, x, group],
                    cx_send.at[p],
                    cx_recv.at[p, g],
                    at_zx(z, to),
                ).start()

    each_part(sums_x, 0, 1)

    mass_part = jnp.zeros((SLICE, LANES), F32)
    for t in range(TILES):
        mass_part += resp[:, t * LANES : (t + 1) * LANES].astype(F32)
    norm_part[...] = mass_part
    block = (NZ * OWN, LANES)
    diagonal = lax.broadcasted_iota(jnp.int32, block, 0) == lax.broadcasted_iota(jnp.int32, block, 1)
    for i in range(NX):
        mass = jnp.sum(norm_part[i * NZ * OWN : (i + 1) * NZ * OWN, :], axis=1, keepdims=True)
        count_send[i] = jnp.sum(jnp.where(diagonal, mass, 0.0), axis=0, keepdims=True)
    for k in (2, 1, 3):
        to = lax.rem(x + k, NX)
        remote(
            count_send.at[to], count_recv.at[x], nx_send.at[0], nx_recv.at[0], at_zx(z, to)
        ).start()
    pending.append(lambda: take(count_recv.at[pl.ds(0, NX - 1)], nx_send.at[0]))
    count_recv[x] = count_send[x]

    each_part(sums_x, 1, PARTS)
    pending.append(lambda: each_part(lambda p: take(sums_recv.at[p, pl.ds(0, NX - 1)], cx_send.at[p])))

    def sums_z(p):
        for g in range(SUM_GROUPS):
            group = slice(g * SUM_PER, (g + 1) * SUM_PER)
            take(sums_recv.at[p, pl.ds(0, NX - 1), pl.ds(g * SUM_PER, SUM_PER)], cx_recv.at[p, g])
            value = sums_f[p, x, group]
            for k in range(1, NX):
                value += sums_recv[p, lax.rem(x + k, NX), group].astype(F32)
            part_send[p, group] = value.astype(BF16)
            for slot in range(g * SUM_PER, (g + 1) * SUM_PER):
                if slot != HOME:
                    remote(
                        part_send.at[p, slot],
                        part_recv.at[p, BACK[slot]],
                        cz_send.at[p],
                        cz_recv.at[p],
                        at_zx(z_peer(slot), x),
                    ).start()
        part_recv[p, HOME] = part_send[p, HOME]

    each_part(sums_z, 0, 2)

    take(count_recv.at[pl.ds(0, NX - 1)], nx_recv.at[0])
    total_send[...] = (count_recv[0] + count_recv[1]) + (count_recv[2] + count_recv[3])
    for slot in range(HOME):
        remote(
            total_send,
            total_recv.at[BACK[slot]],
            nz_send.at[0],
            nz_recv.at[0],
            at_zx(z_peer(slot), x),
        ).start()
    pending.append(lambda: take(total_recv.at[pl.ds(0, NZ - 1)], nz_send.at[0]))
    total_recv[HOME] = total_send[...]

    each_part(sums_z, 2, PARTS)
    pending.append(lambda: each_part(lambda p: take(part_recv.at[p, pl.ds(0, NZ - 1)], cz_send.at[p])))

    norm_part[...] = jnp.zeros_like(norm_part)
    acc[...] = jnp.zeros_like(acc)

    take(total_recv.at[pl.ds(0, NZ - 1)], nz_recv.at[0])
    row = lax.broadcasted_iota(jnp.int32, (OWN, LANES), 0)
    lane = lax.broadcasted_iota(jnp.int32, (OWN, LANES), 1)
    mass = jnp.zeros((OWN, LANES), F32)
    for slot in range(NZ):
        mass += jnp.where(lane == BACK[slot] * OWN + row, total_recv[slot], 0.0)
    mass = jnp.sum(mass, axis=1, keepdims=True) + prior_mass

    def renew(p):
        take(part_recv.at[p, pl.ds(0, NZ - 1)], cz_recv.at[p])
        value = jnp.sum(part_recv[p].astype(F32), axis=0)
        lo = pl.ds(pl.multiple_of(2 * W * p, 2 * W), W)
        hi = pl.ds(pl.multiple_of(2 * W * p + W, W), W)
        left = (value[:OWN] + prior_mass * cent_v[:, lo]) / mass
        right = (value[OWN:] + prior_mass * cent_v[:, hi]) / mass
        upd_out[:, lo] = left
        upd_out[:, hi] = right
        second[p, x, HOME] = jnp.concatenate([left, right], axis=0).astype(BF16)
        spread_z(second, p, uz_send, uz_recv)

    each_part(renew)
    for p in range(PARTS):
        for g in reversed(range(GROUPS)):
            spread_x(second, p, g, ux_send, (uz_recv, ux_recv))
    pending.append(lambda: each_part(lambda p: take(second.at[p, 0, pl.ds(0, NZ - 1)], uz_send.at[p])))
    pending.append(lambda: each_part(lambda p: take(second.at[p, pl.ds(0, NX - 1)], ux_send.at[p])))
    products(second, ux_recv)

    for k in (2, 1, 3, 0):
        chip = lax.rem(y + k, NY)
        for j in range(CHIP_TILES):
            here = pl.ds(pl.multiple_of(chip * CHIP + j * LANES, LANES), LANES)
            score = score_at(here)
            top = jnp.max(score, axis=0, keepdims=True)
            shifted = score - top
            weight = jnp.exp(shifted)
            stat2_send[k, j, 0:1, :] = top
            stat2_send[k, j, 1:2, :] = jnp.sum(weight, axis=0, keepdims=True)
            stat2_send[k, j, 2:3, :] = jnp.sum(weight * shifted, axis=0, keepdims=True)
        targets = (chip * NC + core, chip * NC + 1 - core) if k else (chip * NC + 1 - core,)
        for to in targets:
            remote(
                stat2_send.at[k], stat2_recv.at[cent], st2_send.at[0], st2_recv.at[0], at_cent(to)
            ).start()
    pending.append(lambda: take(stat2_recv.at[pl.ds(0, NCENT - 1)], st2_send.at[0]))
    stat2_recv[cent] = stat2_send[0]
    finish()
    take(stat2_recv.at[pl.ds(0, NCENT - 1)], st2_recv.at[0])
    tops = [stat2_recv[s, :, 0:1, :] for s in range(NCENT)]
    top = tops[0]
    for s in range(1, NCENT):
        top = jnp.maximum(top, tops[s])
    total = jnp.zeros_like(top)
    spread = jnp.zeros_like(top)
    for s in range(NCENT):
        gap = tops[s] - top
        scale = jnp.exp(gap)
        mine = stat2_recv[s, :, 1:2, :]
        total += scale * mine
        spread += scale * (stat2_recv[s, :, 2:3, :] + gap * mine)
    ent_out[...] = jnp.log(total) - spread / total


def on_device(embeddings, centroids):
    vmem = pltpu.VMEM
    dma = pltpu.SemaphoreType.DMA
    gathered = (PARTS, NX, NZ, 2 * OWN, W)
    updated, entropy = pl.pallas_call(
        kernel,
        out_shape=(
            jax.ShapeDtypeStruct((OWN, D), F32),
            jax.ShapeDtypeStruct((CHIP_TILES, 1, LANES), F32),
        ),
        in_specs=[pl.BlockSpec(memory_space=pl.ANY)] * 2,
        out_specs=(pl.BlockSpec(memory_space=vmem), pl.BlockSpec(memory_space=vmem)),
        scratch_shapes=[
            vmem((ROWS, D), F32),
            vmem((OWN, D), F32),
            vmem((GROUP, D), BF16),
            vmem(gathered, BF16),
            vmem(gathered, BF16),
            vmem((SLICE, D), BF16),
            vmem((SLICE, LANES), F32),
            vmem((SLICE, LANES), F32),
            vmem((1, GROUP), F32),
            vmem((SLICE, GROUP), F32),
            vmem((SLICE, GROUP), BF16),
            vmem((2, 2, 8, LANES), F32),
            vmem((2, NCENT, 2, 8, LANES), F32),
            vmem((2, 2, 8, LANES), F32),
            vmem((NY, CHIP_TILES, 8, LANES), F32),
            vmem((NCENT, CHIP_TILES, 8, LANES), F32),
            vmem(gathered, F32),
            vmem(gathered, BF16),
            vmem(gathered, BF16),
            vmem((PARTS, NZ, 2 * OWN, W), BF16),
            vmem((PARTS, NZ, 2 * OWN, W), BF16),
            vmem((NX, 1, LANES), F32),
            vmem((NX, 1, LANES), F32),
            vmem((1, LANES), F32),
            vmem((NZ, 1, LANES), F32),
            dma((2,)),
            dma((14,)),
            dma((NCENT, 2)),
            dma((PARTS,)),
            dma((PARTS, GROUPS)),
            dma((PARTS,)),
            dma((PARTS,)),
            dma((2,)),
            dma((2,)),
            dma((PARTS,)),
            dma((PARTS, SUM_GROUPS)),
            dma((PARTS,)),
            dma((PARTS,)),
            dma((1,)),
            dma((1,)),
            dma((1,)),
            dma((1,)),
            dma((PARTS,)),
            dma((PARTS, GROUPS)),
            dma((PARTS,)),
            dma((PARTS,)),
            dma((1,)),
            dma((1,)),
        ],
        compiler_params=pltpu.CompilerParams(
            collective_id=0, has_side_effects=True, vmem_limit_bytes=63 * 2**20
        ),
        name="em_update",
    )(embeddings, centroids)
    core = lax.axis_index("cent") % NC
    entropy = lax.dynamic_slice_in_dim(entropy.reshape(CHIP), core * ROWS, ROWS, 0)
    return updated, entropy


def solution(mesh):
    in_specs = (P(("dp", "cent"), None), P(("dp", "cent"), None))
    out_specs = (P(("dp", "cent"), None), P(("dp", "cent")))
    return jax.shard_map(
        on_device, mesh=mesh, in_specs=in_specs, out_specs=out_specs, check_vma=False
    )
```
